128 devices in a mesh: seq: 32 (over y, z_lo, x), chan: 4 (over z_hi, core).
Axes of the slice: x: 4, y: 4, z: 4 (z_hi: 2, z_lo: 2; z = z_hi * 2 + z_lo), core: 2. Of those that a mesh axis runs over, the one named last changes fastest.
Arguments:
- base_ids: int32 [1, 32768], P(None, 'seq'), may hold values from 0 to 3
- embedding: bfloat16 [4, 1024], P(None, 'chan'), may hold values from -6 to 6
- gate_values: bfloat16 [1, 32768, 1024], P(None, 'seq', 'chan'), may hold values from -0.03125 to 0.03125
- filter_kernel: bfloat16 [32768, 1024], P('seq', 'chan'), may hold values from -0.03125 to 0.03125
- complement: int32 [1024], replicated, may hold values from 0 to 1023, as said below
- output_gradient: bfloat16 [1, 32768, 1024], P(None, 'seq', 'chan'), may hold values from -6 to 6
Outputs:
- gate_gradient: bfloat16 [1, 32768, 1024], P(None, 'seq', 'chan')
- filter_gradient: float32 [32768, 1024], P('seq', 'chan')
The draws below stay inside these ranges and needn't reach their ends.
Inputs may be any that keep to these rules, and one draw needn't show every extreme that they name: complement[complement[c]] = c and complement[c] != c for every channel c: the channels come in complementary pairs.
All inputs are finite; a program needn't handle non-finite values.
Results may differ from the reference program's by a relative error of at most 0.012.
Values may be sent and summed in bfloat16 or wider, within the bound.
A program may use at most 64 MiB of HBM per device.

```python
import jax
import jax.numpy as jnp
from jax import lax

W = 1024
BATCH = 1
SEQ = 32768


def draw_complement(key, part):
    key = jax.random.fold_in(key, 7)
    shuffled = jax.random.permutation(key, W).astype(jnp.int32)
    partner = shuffled.reshape(W // 2, 2)[:, ::-1].reshape(W)
    return jnp.zeros((W,), jnp.int32).at[shuffled].set(partner)


def set_ends(values, own_key, smallest, top_value):
    place = [jax.random.randint(jax.random.fold_in(own_key, axis), (), 0, length) for axis, length in enumerate(values.shape)]
    widest = values.shape.index(max(values.shape))
    neighbour = place[:widest] + [(place[widest] + 1) % values.shape[widest]] + place[widest + 1:]
    return values.at[tuple(place)].set(smallest).at[tuple(neighbour)].set(top_value)


def levels(stream_key, dims, cuts, least, top_value):
    level = 1.0
    for dim, shards_of in cuts:
        draws = jax.random.uniform(jax.random.fold_in(jax.random.fold_in(stream_key, 6), dim), (shards_of,), jnp.float32, least / len(cuts), top_value / len(cuts))
        level = level * jnp.repeat(jnp.exp(draws), dims[dim] // shards_of).reshape((-1,) + (1,) * (len(dims) - 1 - dim))
    return level


def noise(own_key, extent, spread, bound, split=(), kind=jnp.bfloat16):
    result = spread * jax.random.normal(own_key, extent, jnp.float32)
    if split:
        result = result * levels(own_key, extent, split, -0.22, 0.18)
    return jnp.clip(result, -bound, bound).astype(kind)


def setup_inputs(seed: int = 0) -> dict:
    splits = jax.random.split(jax.random.key(seed), 7)
    base_ids = set_ends(jax.random.randint(splits[0], (BATCH, SEQ), 0, 4), jax.random.fold_in(splits[0], 1), 0, 3).astype(jnp.int32)
    embedding = noise(splits[1], (4, W), 1.0, 6.0, ((1, 4),))
    gate_values = noise(splits[2], (BATCH, SEQ, W), SEQ ** -0.5, 0.03125, ((1, 32), (2, 4)))
    filter_kernel = noise(splits[3], (SEQ, W), SEQ ** -0.5, 0.03125, ((0, 32), (1, 4)))
    complement = draw_complement(jax.random.fold_in(splits[6], 71), 0)
    output_gradient = noise(splits[5], (BATCH, SEQ, W), 1.0, 6.0, ((1, 32), (2, 4)))
    return {"base_ids": base_ids, "embedding": embedding, "gate_values": gate_values, "filter_kernel": filter_kernel, "complement": complement, "output_gradient": output_gradient}


def long_convolution(signal, kernel, complement):
    length = signal.shape[1]
    padded_length = 2 * length
    spectrum = jnp.fft.rfft(kernel, n=padded_length, axis=0)

    def causal(values):
        return jnp.fft.irfft(jnp.fft.rfft(values, n=padded_length, axis=1) * spectrum[None], n=padded_length, axis=1)[:, :length]

    def reverse_complement(values):
        return jnp.take(values[:, ::-1], complement, axis=2)
    return causal(signal) + reverse_complement(causal(reverse_complement(signal)))

def reference(base_ids, embedding, gate_values, filter_kernel, complement, output_gradient):
    letters = jnp.arange(embedding.shape[0], dtype=jnp.int32)
    one_hot = (base_ids[:, :, None] == letters[None, None, :]).astype(jnp.float32)
    embedded = jnp.einsum('btv,vc->btc', one_hot, embedding.astype(jnp.float32))
    conv_input = (gate_values.astype(jnp.float32) * embedded).astype(jnp.bfloat16)
    conv_input = lax.optimization_barrier(conv_input)

    def forward(signal, kernel):
        return long_convolution(signal, kernel, complement)
    _, pullback = jax.vjp(forward, conv_input.astype(jnp.float32), filter_kernel.astype(jnp.float32))
    input_grad, filter_gradient = pullback(output_gradient.astype(jnp.float32))
    gate_gradient = (input_grad * embedded).astype(jnp.bfloat16)
    return (gate_gradient, filter_gradient)
```

```python
import functools
import itertools
import math

import jax
import jax.numpy as jnp
import numpy as np
from jax import lax
from jax.experimental import pallas as pl
from jax.experimental.pallas import tpu as pltpu
from jax.sharding import PartitionSpec as P

MESH = pl.DeviceIdType.MESH
F32 = jnp.float32
BF16 = jnp.bfloat16
SHARDS = 4
SEQ_DEVICES = 32
DEVICES = SHARDS * SEQ_DEVICES
LANES = 128
ROWS = 8
LENGTH = 32768
SHARE = 2 * SHARDS
INNER = 128
OUTER = LENGTH // INNER
HALF = 2 * ROWS
CHANNELS = 256
ALL_CHANNELS = SHARDS * CHANNELS


def two_factors():
    edges = [(a, b) for a in range(SHARDS) for b in range(a, SHARDS)]
    found = []
    for chosen in itertools.combinations_with_replacement(edges, SHARDS):
        degrees = [sum(edge.count(shard) for edge in chosen) for shard in range(SHARDS)]
        if degrees == [2] * SHARDS:
            found.append(chosen)
    return found


def slots_of(chosen):
    used = [0] * SHARDS
    ends = []
    partner = [0] * SHARE
    for a, b in chosen:
        first = used[a]
        used[a] += 1
        second = used[b]
        used[b] += 1
        ends.append((first, second))
        partner[2 * a + first] = 2 * b + second
        partner[2 * b + second] = 2 * a + first
    return ends, partner


FACTORS = [(chosen, *slots_of(chosen)) for chosen in two_factors()]


def split(table):
    high = table.astype(np.float32).astype(jnp.bfloat16)
    low = (table.astype(np.float32) - high.astype(np.float32)).astype(jnp.bfloat16)
    return np.stack([high, low])


def transform_tables():
    window = 2 * LENGTH
    k = np.arange(OUTER)[:, None] + 0.5
    outer_angle = 2 * np.pi * k * np.arange(OUTER)[None] / (2 * OUTER)
    outer = np.concatenate([np.cos(outer_angle), -np.sin(outer_angle)], axis=0)
    m = np.arange(INNER)
    inner_angle = 2 * np.pi * ((m[:, None] * m[None]) % INNER) / INNER
    c, s = np.cos(inner_angle), np.sin(inner_angle)
    inner = np.block([[c, -s], [s, c]])
    twist = 2 * np.pi * k * m[None] / window
    twists = np.stack([np.cos(twist), np.sin(twist)]).astype(np.float32)
    return split(outer), split(outer.T * (2.0 / window)), split(inner), split(inner.T), twists


def device_at(step, seq, chan):
    sy, sz, sx = lax.div(seq, 8), lax.rem(lax.div(seq, 4), 2), lax.rem(seq, 4)
    z = lax.div(chan, 2) * 2 + sz
    core = lax.rem(chan, 2)
    x2 = lax.rem(sx + lax.rem(step, 4), 4)
    y2 = lax.rem(sy + lax.rem(lax.div(step, 4), 4), 4)
    z2 = lax.rem(z + lax.rem(lax.div(step, 16), 4), 4)
    core2 = lax.rem(core + lax.div(step, 64), 2)
    return y2 * 8 + lax.rem(z2, 2) * 4 + x2, lax.div(z2, 2) * 2 + core2


def route(comp_ref, seq, chan, perm_ref):
    comp = comp_ref[...]
    every = lax.broadcasted_iota(jnp.int32, (1, ALL_CHANNELS), 1)
    low, high = jnp.minimum(comp, every), jnp.maximum(comp, every)
    kind = lax.div(low, CHANNELS) * SHARDS + lax.div(high, CHANNELS)
    kind = jnp.where(every < comp, kind, -1)
    kinds = lax.broadcasted_iota(jnp.int32, (16, ALL_CHANNELS), 0)
    hot = jnp.where(kinds == kind, 1.0, 0.0).astype(BF16)
    start = pl.multiple_of(chan * CHANNELS, CHANNELS)
    own_comp = comp_ref[:, pl.ds(start, CHANNELS)]
    own = lax.broadcasted_iota(jnp.int32, (1, CHANNELS), 1) + start
    own_low, own_high = jnp.minimum(own_comp, own), jnp.maximum(own_comp, own)
    own_first = own < own_comp
    own_kind = lax.div(own_low, CHANNELS) * SHARDS + lax.div(own_high, CHANNELS)
    before = lax.broadcasted_iota(jnp.int32, (ALL_CHANNELS, CHANNELS), 0) < own_low
    before = jnp.where(before, 1.0, 0.0).astype(BF16)
    ranks = jnp.dot(hot, before, preferred_element_type=F32)
    own_kinds = lax.broadcasted_iota(jnp.int32, (16, CHANNELS), 0) == own_kind
    rank = jnp.sum(jnp.where(own_kinds, ranks, 0.0), axis=0, keepdims=True)
    totals = jnp.dot(hot, jnp.ones((ALL_CHANNELS, CHANNELS), BF16), preferred_element_type=F32)
    rank = rank.astype(jnp.int32)
    totals = totals.astype(jnp.int32)
    left = {edge: totals[edge[0] * SHARDS + edge[1]][None] for edge in {e for f in FACTORS for e in f[0]}}
    taken = {edge: jnp.zeros((1, CHANNELS), jnp.int32) for edge in left}
    begin = jnp.zeros((1, CHANNELS), jnp.int32)
    me = chan * SEQ_DEVICES + seq
    place = jnp.zeros((1, CHANNELS), jnp.int32)
    code = jnp.zeros((1, CHANNELS), jnp.int32)
    for chosen, ends, partner in FACTORS:
        count = None
        for edge in set(chosen):
            possible = left[edge] if chosen.count(edge) == 1 else lax.shift_right_logical(left[edge], 1)
            count = possible if count is None else jnp.minimum(count, possible)
        for edge in sorted(set(chosen)):
            times = chosen.count(edge)
            first, second = ends[chosen.index(edge)]
            offset = rank - taken[edge]
            size = count * times
            here = (own_kind == edge[0] * SHARDS + edge[1]) & (offset >= 0) & (offset < size)
            if times == 2:
                spot = 2 * begin + offset
            else:
                spot = 2 * (begin + offset) + jnp.where(own_first, first, second)
            place = jnp.where(here, spot, place)
            left[edge] = left[edge] - size
            taken[edge] = taken[edge] + size
        mine = (begin <= me) & (me < begin + count)
        code = jnp.where(mine, sum(p << (3 * i) for i, p in enumerate(partner)), code)
        begin = begin + count
    slots = lax.broadcasted_iota(jnp.int32, (CHANNELS, CHANNELS), 0)
    perm_ref[...] = jnp.where(slots == place, 1.0, 0.0).astype(BF16)
    return jnp.max(code)


def kernel(
    ids_hbm, emb_hbm, gate_hbm, filt_hbm, comp_hbm, grad_hbm,
    outer_hbm, outer_back_hbm, inner_hbm, inner_back_hbm, twist_hbm,
    gate_out, filt_out,
    ids, emb, gate, filt, comp, grad,
    outer, outer_back, inner, inner_back, twist,
    perm, strided, letters, embedded, spectra,
    send_k, send_g, send_u, recv_k, recv_g, recv_u,
    send_du, send_dk, recv_du, recv_dk, gate_vmem, filt_vmem,
    load_sem, store_sem, local_sem, send_sem, recv_sem,
):
    seq, chan = lax.axis_index("seq"), lax.axis_index("chan")
    me = chan * SEQ_DEVICES + seq
    loads = {}
    sources = [
        (comp_hbm, comp), (ids_hbm, ids), (emb_hbm, emb), (filt_hbm, filt), (grad_hbm, grad), (gate_hbm, gate),
        (outer_hbm, outer), (twist_hbm, twist), (inner_hbm, inner), (inner_back_hbm, inner_back),
        (outer_back_hbm, outer_back),
    ]
    for index, (source, target) in enumerate(sources):
        loads[index] = pltpu.make_async_copy(source, target, load_sem.at[index])
        loads[index].start()

    barrier = pltpu.get_barrier_semaphore()

    def greet(step, carry):
        pl.semaphore_signal(barrier, inc=1, device_id=device_at(step, seq, chan), device_id_type=MESH)
        return carry

    lax.fori_loop(1, DEVICES, greet, 0)

    loads[0].wait()
    code = route(comp, seq, chan, perm)

    def lay_out(source_of, target):
        for a in range(ROWS):
            strided[pl.ds(a, CHANNELS, stride=ROWS), :] = source_of(a)
        target[...] = strided[...].reshape(DEVICES, HALF, LANES).astype(BF16)

    def turned(ref):
        def part(a):
            block = ref[pl.ds(a * LANES, LANES), :]
            return lax.dot_general(perm[...], block, (((1,), (1,)), ((), ())), preferred_element_type=F32)
        return part

    def post(source, target, index):
        pltpu.make_async_copy(source.at[me], target.at[me], local_sem.at[index]).start()

        def one(step, carry):
            seq2, chan2 = device_at(lax.rem(step * 37, DEVICES), seq, chan)
            pltpu.make_async_remote_copy(
                source.at[chan2 * SEQ_DEVICES + seq2], target.at[me], send_sem.at[index], recv_sem.at[index],
                device_id=(seq2, chan2), device_id_type=MESH,
            ).start()
            return carry

        lax.fori_loop(1, DEVICES, one, 0)

    def arrived(source, target, index):
        pltpu.make_async_copy(source.at[me], target.at[me], local_sem.at[index]).wait()
        rest = pl.ds(0, DEVICES - 1)
        pltpu.make_async_copy(target.at[rest], target.at[rest], recv_sem.at[index]).wait()

    def left_here(source, index):
        rest = pl.ds(0, DEVICES - 1)
        pltpu.make_async_copy(source.at[rest], source.at[rest], send_sem.at[index]).wait()

    loads[3].wait()
    lay_out(turned(filt), send_k)
    pl.semaphore_wait(barrier, DEVICES - 1)
    post(send_k, recv_k, 0)

    loads[4].wait()
    lay_out(turned(grad), send_g)
    post(send_g, recv_g, 1)

    loads[1].wait()
    loads[2].wait()
    names = lax.broadcasted_iota(jnp.int32, (4, ALL_CHANNELS), 0)
    letters[...] = jnp.where(names == ids[...], 1.0, 0.0).astype(BF16)
    own_emb = lax.dot_general(perm[...], emb[...], (((1,), (1,)), ((), ())), preferred_element_type=F32).astype(BF16)
    for a in range(ROWS):
        embedded[a] = jnp.dot(own_emb, letters[:, a * LANES : (a + 1) * LANES], preferred_element_type=F32)
    loads[5].wait()
    turn_gate = turned(gate)
    lay_out(lambda a: turn_gate(a) * embedded[a], send_u)
    post(send_u, recv_u, 2)

    for index in range(6, 11):
        loads[index].wait()

    def times(matrices, right):
        return jnp.dot(matrices[0], right, preferred_element_type=F32) + jnp.dot(
            matrices[1], right, preferred_element_type=F32
        )

    def times_right(left, matrices):
        return jnp.dot(left, matrices[0], preferred_element_type=F32) + jnp.dot(
            left, matrices[1], preferred_element_type=F32
        )

    def forward(received, shard):
        block = received[pl.ds(shard * SEQ_DEVICES, SEQ_DEVICES)].astype(F32)
        block = block.reshape(SEQ_DEVICES, 2, ROWS, LANES)
        fields = [block[:, slot].reshape(OUTER, INNER) for slot in range(2)]
        mixed = times(outer, jnp.concatenate(fields, axis=1).astype(BF16))
        cos, sin = twist[0], twist[1]
        spread = []
        for slot in range(2):
            real = mixed[:OUTER, slot * INNER : (slot + 1) * INNER]
            imag = mixed[OUTER:, slot * INNER : (slot + 1) * INNER]
            spread.append(jnp.concatenate([real * cos + imag * sin, imag * cos - real * sin], axis=1))
        return times_right(jnp.concatenate(spread, axis=0).astype(BF16), inner)

    def backward(parts):
        rows = [jnp.concatenate([real, imag], axis=1) for real, imag in parts]
        mixed = times_right(jnp.concatenate(rows, axis=0).astype(BF16), inner_back)
        cos, sin = twist[0], twist[1]
        spread = []
        for slot in range(2):
            real = mixed[slot * OUTER : (slot + 1) * OUTER, :INNER]
            imag = mixed[slot * OUTER : (slot + 1) * OUTER, INNER:]
            spread.append(jnp.concatenate([real * cos - imag * sin, imag * cos + real * sin], axis=0))
        fields = times(outer_back, jnp.concatenate(spread, axis=1).astype(BF16))
        halves = [
            fields[:, slot * INNER : (slot + 1) * INNER].reshape(SEQ_DEVICES, 1, ROWS, LANES) for slot in range(2)
        ]
        return jnp.concatenate(halves, axis=1).reshape(SEQ_DEVICES, HALF, LANES).astype(BF16)

    def spectrum(kind, channel):
        both = spectra[kind * SHARE + channel]
        return both[:, :INNER], both[:, INNER:]

    def partner_of(channel):
        return lax.rem(lax.shift_right_logical(code, 3 * channel), SHARE)

    def all_forward(received, kind, finish):
        def body(shard, carry):
            both = forward(received, shard)
            for slot in range(2):
                channel = 2 * shard + slot
                spectra[kind * SHARE + channel] = finish(both[slot * OUTER : (slot + 1) * OUTER], channel)
            return carry

        lax.fori_loop(0, SHARDS, body, 0)

    def all_backward(combine, source, target, index):
        pltpu_local = pltpu.make_async_copy(source.at[me], target.at[me], local_sem.at[index])

        def body(turn, carry):
            shard = lax.rem(chan + turn, SHARDS)
            base = shard * SEQ_DEVICES
            source[pl.ds(base, SEQ_DEVICES)] = backward([combine(2 * shard + slot) for slot in range(2)])

            @pl.when(turn == 0)
            def _():
                pltpu_local.start()

            def one(step, inner_carry):
                seq2 = lax.rem(seq + step, SEQ_DEVICES)
                pltpu.make_async_remote_copy(
                    source.at[base + seq2], target.at[me], send_sem.at[index], recv_sem.at[index],
                    device_id=(seq2, shard), device_id_type=MESH,
                ).start()
                return inner_carry

            lax.fori_loop(jnp.where(turn == 0, 1, 0), SEQ_DEVICES, one, 0)
            return carry

        lax.fori_loop(0, SHARDS, body, 0)

    arrived(send_k, recv_k, 0)
    all_forward(recv_k, 0, lambda both, channel: both)
    arrived(send_g, recv_g, 1)
    all_forward(recv_g, 1, lambda both, channel: both)

    def input_spectrum(channel):
        k_real, k_imag = spectrum(0, channel)
        p_real, p_imag = spectrum(0, partner_of(channel))
        g_real, g_imag = spectrum(1, channel)
        real, imag = k_real + p_real, p_imag - k_imag
        return g_real * real - g_imag * imag, g_real * imag + g_imag * real

    all_backward(input_spectrum, send_du, recv_du, 3)

    def product(both, channel):
        g_real, g_imag = spectrum(1, channel)
        u_real, u_imag = both[:, :INNER], both[:, INNER:]
        return jnp.concatenate([g_real * u_real + g_imag * u_imag, g_imag * u_real - g_real * u_imag], axis=1)

    arrived(send_u, recv_u, 2)
    all_forward(recv_u, 2, product)

    def filter_spectrum(channel):
        real, imag = spectrum(2, channel)
        p_real, p_imag = spectrum(2, partner_of(channel))
        return real + p_real, imag - p_imag

    all_backward(filter_spectrum, send_dk, recv_dk, 4)

    def give_back(received, scale, target):
        strided[...] = received[...].astype(F32).reshape(DEVICES * HALF, LANES)
        for a in range(ROWS):
            part = scale(strided[pl.ds(a, CHANNELS, stride=ROWS), :], a).astype(BF16)
            block = lax.dot_general(part, perm[...], (((0,), (0,)), ((), ())), preferred_element_type=F32)
            target[pl.ds(a * LANES, LANES), :] = block.astype(target.dtype)

    arrived(send_du, recv_du, 3)
    give_back(recv_du, lambda part, a: part * embedded[a], gate_vmem)
    gate_store = pltpu.make_async_copy(gate_vmem, gate_out, store_sem.at[0])
    gate_store.start()
    arrived(send_dk, recv_dk, 4)
    give_back(recv_dk, lambda part, a: part, filt_vmem)
    filt_store = pltpu.make_async_copy(filt_vmem, filt_out, store_sem.at[1])
    filt_store.start()
    for index, source in enumerate([send_k, send_g, send_u, send_du, send_dk]):
        left_here(source, index)
    gate_store.wait()
    filt_store.wait()


def shards(base_ids, embedding, gate_values, filter_kernel, complement, output_gradient):
    positions, channels = filter_kernel.shape
    tables = transform_tables()
    blocks = pltpu.VMEM((DEVICES, HALF, LANES), BF16)
    gate_gradient, filter_gradient = pl.pallas_call(
        kernel,
        out_shape=[
            jax.ShapeDtypeStruct((positions, channels), BF16),
            jax.ShapeDtypeStruct((positions, channels), F32),
        ],
        in_specs=[pl.BlockSpec(memory_space=pl.ANY)] * 11,
        out_specs=[pl.BlockSpec(memory_space=pl.ANY)] * 2,
        scratch_shapes=[
            pltpu.VMEM((1, positions), jnp.int32),
            pltpu.VMEM(embedding.shape, BF16),
            pltpu.VMEM((positions, channels), BF16),
            pltpu.VMEM((positions, channels), BF16),
            pltpu.VMEM((1, ALL_CHANNELS), jnp.int32),
            pltpu.VMEM((positions, channels), BF16),
            *[pltpu.VMEM(table.shape, table.dtype) for table in tables],
            pltpu.VMEM((channels, channels), BF16),
            pltpu.VMEM((DEVICES * HALF, LANES), F32),
            pltpu.VMEM((4, positions), BF16),
            pltpu.VMEM((ROWS, channels, LANES), F32),
            pltpu.VMEM((3 * SHARE, OUTER, 2 * INNER), F32),
            *[blocks] * 10,
            pltpu.VMEM((positions, channels), BF16),
            pltpu.VMEM((positions, channels), F32),
            pltpu.SemaphoreType.DMA((11,)),
            pltpu.SemaphoreType.DMA((2,)),
            pltpu.SemaphoreType.DMA((5,)),
            pltpu.SemaphoreType.DMA((5,)),
            pltpu.SemaphoreType.DMA((5,)),
        ],
        compiler_params=pltpu.CompilerParams(collective_id=0, has_side_effects=True, vmem_limit_bytes=48 << 20),
        name="two_strand_gradients",
    )(
        base_ids, embedding, gate_values.reshape(positions, channels), filter_kernel,
        complement.reshape(1, -1), output_gradient.reshape(positions, channels),
        *[jnp.asarray(table) for table in tables],
    )
    return gate_gradient[None], filter_gradient


def solution(mesh):
    in_specs = (
        P(None, "seq"),
        P(None, "chan"),
        P(None, "seq", "chan"),
        P("seq", "chan"),
        P(),
        P(None, "seq", "chan"),
    )
    out_specs = (P(None, "seq", "chan"), P("seq", "chan"))
    return jax.shard_map(shards, mesh=mesh, in_specs=in_specs, out_specs=out_specs, check_vma=False)
```

```python
import functools
import itertools
import math

import jax
import jax.numpy as jnp
import numpy as np
from jax import lax
from jax.experimental import pallas as pl
from jax.experimental.pallas import tpu as pltpu
from jax.sharding import PartitionSpec as P

MESH = pl.DeviceIdType.MESH
F32 = jnp.float32
BF16 = jnp.bfloat16
SHARDS = 4
SEQ_DEVICES = 32
DEVICES = SHARDS * SEQ_DEVICES
LANES = 128
ROWS = 8
LENGTH = 32768
SHARE = 2 * SHARDS
INNER = 128
OUTER = LENGTH // INNER
HALF = 2 * ROWS
CHANNELS = 256
ALL_CHANNELS = SHARDS * CHANNELS
UNROLL = 1


def two_factors():
    edges = [(a, b) for a in range(SHARDS) for b in range(a, SHARDS)]
    found = []
    for chosen in itertools.combinations_with_replacement(edges, SHARDS):
        degrees = [sum(edge.count(shard) for edge in chosen) for shard in range(SHARDS)]
        if degrees == [2] * SHARDS:
            found.append(chosen)
    return found


def slots_of(chosen):
    used = [0] * SHARDS
    ends = []
    partner = [0] * SHARE
    for a, b in chosen:
        first = used[a]
        used[a] += 1
        second = used[b]
        used[b] += 1
        ends.append((first, second))
        partner[2 * a + first] = 2 * b + second
        partner[2 * b + second] = 2 * a + first
    return ends, partner


FACTORS = [(chosen, *slots_of(chosen)) for chosen in two_factors()]


def split(table):
    high = table.astype(np.float32).astype(jnp.bfloat16)
    low = (table.astype(np.float32) - high.astype(np.float32)).astype(jnp.bfloat16)
    return np.stack([high, low])


def transform_tables():
    window = 2 * LENGTH
    k = np.arange(OUTER)[:, None] + 0.5
    outer_angle = 2 * np.pi * k * np.arange(OUTER)[None] / (2 * OUTER)
    outer = np.concatenate([np.cos(outer_angle), -np.sin(outer_angle)], axis=0)
    m = np.arange(INNER)
    inner_angle = 2 * np.pi * ((m[:, None] * m[None]) % INNER) / INNER
    c, s = np.cos(inner_angle), np.sin(inner_angle)
    inner = np.block([[c, -s], [s, c]])
    twist = 2 * np.pi * k * m[None] / window
    twists = np.stack([np.cos(twist), np.sin(twist)]).astype(np.float32)
    return split(outer), split(outer.T * (2.0 / window)), split(inner), split(inner.T), twists


FAR_FIRST = (2, 1, 3, 0)


class Neighbours:
    def __init__(self, seq, chan):
        self.sy, self.sz, self.sx = lax.div(seq, 8), lax.rem(lax.div(seq, 4), 2), lax.rem(seq, 4)
        self.sz_high, self.core = lax.div(chan, 2), lax.rem(chan, 2)
        self.x = [lax.rem(self.sx + step, 4) for step in range(4)]
        self.y = [lax.rem(self.sy + step, 4) * 8 for step in range(4)]
        self.z_low = [lax.rem(self.sz + step, 2) * 4 for step in range(2)]

    def layer(self, step):
        z = lax.rem(self.sz_high * 2 + self.sz + lax.rem(step, 4), 4)
        core = lax.rem(self.core + lax.div(step, 4), 2)
        return lax.rem(z, 2) * 4, lax.div(z, 2) * 2 + core

    def each_other(self, visit):
        def around(step, own):
            low, chan = self.layer(step)
            for dy in FAR_FIRST:
                for dx in FAR_FIRST:
                    if not (own and dx == 0 and dy == 0):
                        visit(self.y[dy] + low + self.x[dx], chan)

        def body(step, carry):
            around(step, False)
            return carry

        lax.fori_loop(1, 8, body, 0)
        around(0, True)

    def each_in_shard(self, visit):
        for low in (1, 0):
            for dy in FAR_FIRST:
                for dx in FAR_FIRST:
                    visit(self.y[dy] + self.z_low[low] + self.x[dx], low == 0 and dx == 0 and dy == 0)


def route(comp_ref, seq, chan, perm_ref):
    comp = comp_ref[...]
    every = lax.broadcasted_iota(jnp.int32, (1, ALL_CHANNELS), 1)
    low, high = jnp.minimum(comp, every), jnp.maximum(comp, every)
    kind = lax.div(low, CHANNELS) * SHARDS + lax.div(high, CHANNELS)
    kind = jnp.where(every < comp, kind, -1)
    kinds = lax.broadcasted_iota(jnp.int32, (16, ALL_CHANNELS), 0)
    hot = jnp.where(kinds == kind, 1.0, 0.0).astype(BF16)
    start = pl.multiple_of(chan * CHANNELS, CHANNELS)
    own_comp = comp_ref[:, pl.ds(start, CHANNELS)]
    own = lax.broadcasted_iota(jnp.int32, (1, CHANNELS), 1) + start
    own_low, own_high = jnp.minimum(own_comp, own), jnp.maximum(own_comp, own)
    own_first = own < own_comp
    own_kind = lax.div(own_low, CHANNELS) * SHARDS + lax.div(own_high, CHANNELS)
    before = lax.broadcasted_iota(jnp.int32, (ALL_CHANNELS, CHANNELS), 0) < own_low
    before = jnp.where(before, 1.0, 0.0).astype(BF16)
    ranks = jnp.dot(hot, before, preferred_element_type=F32)
    own_kinds = lax.broadcasted_iota(jnp.int32, (16, CHANNELS), 0) == own_kind
    rank = jnp.sum(jnp.where(own_kinds, ranks, 0.0), axis=0, keepdims=True)
    totals = jnp.dot(hot, jnp.ones((ALL_CHANNELS, CHANNELS), BF16), preferred_element_type=F32)
    rank = rank.astype(jnp.int32)
    totals = totals.astype(jnp.int32)
    left = {edge: totals[edge[0] * SHARDS + edge[1]][None] for edge in sorted({e for f in FACTORS for e in f[0]})}
    taken = {edge: jnp.zeros((1, CHANNELS), jnp.int32) for edge in left}
    begin = jnp.zeros((1, CHANNELS), jnp.int32)
    me = chan * SEQ_DEVICES + seq
    place = jnp.zeros((1, CHANNELS), jnp.int32)
    code = jnp.zeros((1, CHANNELS), jnp.int32)
    for chosen, ends, partner in FACTORS:
        count = None
        for edge in sorted(set(chosen)):
            possible = left[edge] if chosen.count(edge) == 1 else lax.shift_right_logical(left[edge], 1)
            count = possible if count is None else jnp.minimum(count, possible)
        for edge in sorted(set(chosen)):
            times = chosen.count(edge)
            first, second = ends[chosen.index(edge)]
            offset = rank - taken[edge]
            size = count * times
            here = (own_kind == edge[0] * SHARDS + edge[1]) & (offset >= 0) & (offset < size)
            if times == 2:
                spot = 2 * begin + offset
            else:
                spot = 2 * (begin + offset) + jnp.where(own_first, first, second)
            place = jnp.where(here, spot, place)
            left[edge] = left[edge] - size
            taken[edge] = taken[edge] + size
        mine = (begin <= me) & (me < begin + count)
        code = jnp.where(mine, sum(p << (3 * i) for i, p in enumerate(partner)), code)
        begin = begin + count
    slots = lax.broadcasted_iota(jnp.int32, (CHANNELS, CHANNELS), 0)
    perm_ref[...] = jnp.where(slots == place, 1.0, 0.0).astype(BF16)
    return jnp.max(code)


def kernel(
    ids_hbm, emb_hbm, gate_hbm, filt_hbm, comp_hbm, grad_hbm,
    outer_hbm, outer_back_hbm, inner_hbm, inner_back_hbm, twist_hbm,
    gate_out, filt_out,
    ids, emb, gate, filt, comp, grad,
    outer, outer_back, inner, inner_back, twist,
    perm, strided, letters, embedded, spectra_k, spectra_g, spectra_u,
    send_k, send_g, send_u, recv_k, recv_g, recv_u,
    send_du, send_dk, recv_du, recv_dk, gate_vmem, filt_vmem,
    load_sem, store_sem, local_sem, send_sem, recv_sem,
):
    spectra = (spectra_k, spectra_g, spectra_u)
    seq, chan = lax.axis_index("seq"), lax.axis_index("chan")
    me = chan * SEQ_DEVICES + seq
    loads = {}
    sources = [
        (comp_hbm, comp), (ids_hbm, ids), (emb_hbm, emb), (filt_hbm, filt), (grad_hbm, grad), (gate_hbm, gate),
        (outer_hbm, outer), (twist_hbm, twist), (inner_hbm, inner), (inner_back_hbm, inner_back),
        (outer_back_hbm, outer_back),
    ]
    for index, (source, target) in enumerate(sources):
        loads[index] = pltpu.make_async_copy(source, target, load_sem.at[index])
        loads[index].start()

    barrier = pltpu.get_barrier_semaphore()

    near = Neighbours(seq, chan)
    near.each_other(
        lambda seq2, chan2: pl.semaphore_signal(barrier, inc=1, device_id=(seq2, chan2), device_id_type=MESH)
    )

    loads[0].wait()
    code = route(comp, seq, chan, perm)

    def lay_out(source_of, target):
        for a in range(ROWS):
            strided[pl.ds(a, CHANNELS, stride=ROWS), :] = source_of(a)
        target[...] = strided[...].reshape(DEVICES, HALF, LANES).astype(BF16)

    def turned(ref):
        def part(a):
            block = ref[pl.ds(a * LANES, LANES), :]
            return lax.dot_general(perm[...], block, (((1,), (1,)), ((), ())), preferred_element_type=F32)
        return part

    def post(source, target, index):
        pltpu.make_async_copy(source.at[me], target.at[me], local_sem.at[index]).start()

        def one(seq2, chan2):
            pltpu.make_async_remote_copy(
                source.at[chan2 * SEQ_DEVICES + seq2], target.at[me], send_sem.at[index], recv_sem.at[index],
                device_id=(seq2, chan2), device_id_type=MESH,
            ).start()

        near.each_other(one)

    def arrived(source, target, index):
        pltpu.make_async_copy(source.at[me], target.at[me], local_sem.at[index]).wait()
        rest = pl.ds(0, DEVICES - 1)
        pltpu.make_async_copy(target.at[rest], target.at[rest], recv_sem.at[index]).wait()

    def left_here(source, index):
        rest = pl.ds(0, DEVICES - 1)
        pltpu.make_async_copy(source.at[rest], source.at[rest], send_sem.at[index]).wait()

    loads[3].wait()
    lay_out(turned(filt), send_k)
    pl.semaphore_wait(barrier, DEVICES - 1)
    post(send_k, recv_k, 0)

    loads[4].wait()
    lay_out(turned(grad), send_g)
    post(send_g, recv_g, 1)

    loads[1].wait()
    loads[2].wait()
    names = lax.broadcasted_iota(jnp.int32, (4, ALL_CHANNELS), 0)
    letters[...] = jnp.where(names == ids[...], 1.0, 0.0).astype(BF16)
    own_emb = lax.dot_general(perm[...], emb[...], (((1,), (1,)), ((), ())), preferred_element_type=F32).astype(BF16)
    for a in range(ROWS):
        embedded[a] = jnp.dot(own_emb, letters[:, a * LANES : (a + 1) * LANES], preferred_element_type=F32)
    loads[5].wait()
    turn_gate = turned(gate)
    lay_out(lambda a: turn_gate(a) * embedded[a], send_u)
    post(send_u, recv_u, 2)

    for index in range(6, 11):
        loads[index].wait()

    def times(matrices, right):
        return jnp.dot(matrices[0], right, preferred_element_type=F32) + jnp.dot(
            matrices[1], right, preferred_element_type=F32
        )

    def times_right(left, matrices):
        return jnp.dot(left, matrices[0], preferred_element_type=F32) + jnp.dot(
            left, matrices[1], preferred_element_type=F32
        )

    def forward(received, shard):
        block = received[pl.ds(shard * SEQ_DEVICES, SEQ_DEVICES)].astype(F32)
        block = block.reshape(SEQ_DEVICES, 2, ROWS, LANES)
        fields = [block[:, slot].reshape(OUTER, INNER) for slot in range(2)]
        mixed = times(outer, jnp.concatenate(fields, axis=1).astype(BF16))
        cos, sin = twist[0], twist[1]
        spread = []
        for slot in range(2):
            real = mixed[:OUTER, slot * INNER : (slot + 1) * INNER]
            imag = mixed[OUTER:, slot * INNER : (slot + 1) * INNER]
            spread.append(jnp.concatenate([real * cos + imag * sin, imag * cos - real * sin], axis=1))
        return times_right(jnp.concatenate(spread, axis=0).astype(BF16), inner)

    def backward(parts):
        rows = [jnp.concatenate([real, imag], axis=1) for real, imag in parts]
        mixed = times_right(jnp.concatenate(rows, axis=0).astype(BF16), inner_back)
        cos, sin = twist[0], twist[1]
        spread = []
        for slot in range(2):
            real = mixed[slot * OUTER : (slot + 1) * OUTER, :INNER]
            imag = mixed[slot * OUTER : (slot + 1) * OUTER, INNER:]
            spread.append(jnp.concatenate([real * cos - imag * sin, imag * cos + real * sin], axis=0))
        fields = times(outer_back, jnp.concatenate(spread, axis=1).astype(BF16))
        halves = [
            fields[:, slot * INNER : (slot + 1) * INNER].reshape(SEQ_DEVICES, 1, ROWS, LANES) for slot in range(2)
        ]
        return jnp.concatenate(halves, axis=1).reshape(SEQ_DEVICES, HALF, LANES).astype(BF16)

    def spectrum(kind, channel):
        both = spectra[kind][channel]
        return both[:, :INNER], both[:, INNER:]

    def partner_of(channel):
        return lax.rem(lax.shift_right_logical(code, 3 * channel), SHARE)

    def forward_shard(received, kind, finish, shard):
        both = forward(received, shard)
        for slot in range(2):
            channel = 2 * shard + slot
            spectra[kind][channel] = finish(both[slot * OUTER : (slot + 1) * OUTER], channel)

    def all_forward(received, kind, finish):
        def body(shard, carry):
            forward_shard(received, kind, finish, shard)
            return carry

        lax.fori_loop(0, SHARDS, body, 0, unroll=UNROLL)

    def all_backward(prepare, combine, source, target, index):
        def body(turn, carry):
            shard = lax.rem(chan + 1 + turn, SHARDS)
            base = shard * SEQ_DEVICES
            prepare(shard)
            source[pl.ds(base, SEQ_DEVICES)] = backward([combine(2 * shard + slot) for slot in range(2)])

            def one(seq2, own):
                def other():
                    pltpu.make_async_remote_copy(
                        source.at[base + seq2], target.at[me], send_sem.at[index], recv_sem.at[index],
                        device_id=(seq2, shard), device_id_type=MESH,
                    ).start()

                if own:
                    pl.when(turn < SHARDS - 1)(other)
                else:
                    other()

            near.each_in_shard(one)
            return carry

        lax.fori_loop(0, SHARDS, body, 0)
        pltpu.make_async_copy(source.at[me], target.at[me], local_sem.at[index]).start()

    arrived(send_k, recv_k, 0)
    all_forward(recv_k, 0, lambda both, channel: both)
    arrived(send_g, recv_g, 1)

    def input_spectrum(channel):
        k_real, k_imag = spectrum(0, channel)
        p_real, p_imag = spectrum(0, partner_of(channel))
        g_real, g_imag = spectrum(1, channel)
        real, imag = k_real + p_real, p_imag - k_imag
        return g_real * real - g_imag * imag, g_real * imag + g_imag * real

    all_backward(
        lambda shard: forward_shard(recv_g, 1, lambda both, channel: both, shard), input_spectrum, send_du, recv_du, 3
    )

    def product(both, channel):
        g_real, g_imag = spectrum(1, channel)
        u_real, u_imag = both[:, :INNER], both[:, INNER:]
        return jnp.concatenate([g_real * u_real + g_imag * u_imag, g_imag * u_real - g_real * u_imag], axis=1)

    arrived(send_u, recv_u, 2)
    all_forward(recv_u, 2, product)

    def filter_spectrum(channel):
        real, imag = spectrum(2, channel)
        p_real, p_imag = spectrum(2, partner_of(channel))
        return real + p_real, imag - p_imag

    all_backward(lambda shard: None, filter_spectrum, send_dk, recv_dk, 4)

    def give_back(received, scale, target):
        strided[...] = received[...].astype(F32).reshape(DEVICES * HALF, LANES)
        for a in range(ROWS):
            part = scale(strided[pl.ds(a, CHANNELS, stride=ROWS), :], a).astype(BF16)
            block = lax.dot_general(part, perm[...], (((0,), (0,)), ((), ())), preferred_element_type=F32)
            target[pl.ds(a * LANES, LANES), :] = block.astype(target.dtype)

    arrived(send_du, recv_du, 3)
    give_back(recv_du, lambda part, a: part * embedded[a], gate_vmem)
    gate_store = pltpu.make_async_copy(gate_vmem, gate_out, store_sem.at[0])
    gate_store.start()
    arrived(send_dk, recv_dk, 4)
    give_back(recv_dk, lambda part, a: part, filt_vmem)
    filt_store = pltpu.make_async_copy(filt_vmem, filt_out, store_sem.at[1])
    filt_store.start()
    for index, source in enumerate([send_k, send_g, send_u, send_du, send_dk]):
        left_here(source, index)
    gate_store.wait()
    filt_store.wait()


def shards(base_ids, embedding, gate_values, filter_kernel, complement, output_gradient):
    positions, channels = filter_kernel.shape
    tables = transform_tables()
    blocks = pltpu.VMEM((DEVICES, HALF, LANES), BF16)
    gate_gradient, filter_gradient = pl.pallas_call(
        kernel,
        out_shape=[
            jax.ShapeDtypeStruct((positions, channels), BF16),
            jax.ShapeDtypeStruct((positions, channels), BF16),
        ],
        in_specs=[pl.BlockSpec(memory_space=pl.ANY)] * 11,
        out_specs=[pl.BlockSpec(memory_space=pl.ANY)] * 2,
        scratch_shapes=[
            pltpu.VMEM((1, positions), jnp.int32),
            pltpu.VMEM(embedding.shape, BF16),
            pltpu.VMEM((positions, channels), BF16),
            pltpu.VMEM((positions, channels), BF16),
            pltpu.VMEM((1, ALL_CHANNELS), jnp.int32),
            pltpu.VMEM((positions, channels), BF16),
            *[pltpu.VMEM(table.shape, table.dtype) for table in tables],
            pltpu.VMEM((channels, channels), BF16),
            pltpu.VMEM((DEVICES * HALF, LANES), F32),
            pltpu.VMEM((4, positions), BF16),
            pltpu.VMEM((ROWS, channels, LANES), F32),
            *[pltpu.VMEM((SHARE, OUTER, 2 * INNER), F32)] * 3,
            *[blocks] * 10,
            pltpu.VMEM((positions, channels), BF16),
            pltpu.VMEM((positions, channels), BF16),
            pltpu.SemaphoreType.DMA((11,)),
            pltpu.SemaphoreType.DMA((2,)),
            pltpu.SemaphoreType.DMA((5,)),
            pltpu.SemaphoreType.DMA((5,)),
            pltpu.SemaphoreType.DMA((5,)),
        ],
        compiler_params=pltpu.CompilerParams(collective_id=0, has_side_effects=True, vmem_limit_bytes=62 << 20),
        name="two_strand_gradients",
    )(
        base_ids, embedding, gate_values.reshape(positions, channels), filter_kernel,
        complement.reshape(1, -1), output_gradient.reshape(positions, channels),
        *[jnp.asarray(table) for table in tables],
    )
    return gate_gradient[None], filter_gradient.astype(F32)


def solution(mesh):
    in_specs = (
        P(None, "seq"),
        P(None, "chan"),
        P(None, "seq", "chan"),
        P("seq", "chan"),
        P(),
        P(None, "seq", "chan"),
    )
    out_specs = (P(None, "seq", "chan"), P("seq", "chan"))
    return jax.shard_map(shards, mesh=mesh, in_specs=in_specs, out_specs=out_specs, check_vma=False)
```

```python
import functools
import itertools
import math

import jax
import jax.numpy as jnp
import numpy as np
from jax import lax
from jax.experimental import pallas as pl
from jax.experimental.pallas import tpu as pltpu
from jax.sharding import PartitionSpec as P

MESH = pl.DeviceIdType.MESH
F32 = jnp.float32
BF16 = jnp.bfloat16
SHARDS = 4
SEQ_DEVICES = 32
DEVICES = SHARDS * SEQ_DEVICES
LANES = 128
ROWS = 8
LENGTH = 32768
SHARE = 2 * SHARDS
INNER = 128
OUTER = LENGTH // INNER
HALF = 2 * ROWS
CHANNELS = 256
ALL_CHANNELS = SHARDS * CHANNELS
UNROLL = 4


def two_factors():
    edges = [(a, b) for a in range(SHARDS) for b in range(a, SHARDS)]
    found = []
    for chosen in itertools.combinations_with_replacement(edges, SHARDS):
        degrees = [sum(edge.count(shard) for edge in chosen) for shard in range(SHARDS)]
        if degrees == [2] * SHARDS:
            found.append(chosen)
    return found


def slots_of(chosen):
    used = [0] * SHARDS
    ends = []
    partner = [0] * SHARE
    for a, b in chosen:
        first = used[a]
        used[a] += 1
        second = used[b]
        used[b] += 1
        ends.append((first, second))
        partner[2 * a + first] = 2 * b + second
        partner[2 * b + second] = 2 * a + first
    return ends, partner


FACTORS = [(chosen, *slots_of(chosen)) for chosen in two_factors()]


def split(table):
    high = table.astype(np.float32).astype(jnp.bfloat16)
    low = (table.astype(np.float32) - high.astype(np.float32)).astype(jnp.bfloat16)
    return np.stack([high, low])


def transform_tables():
    window = 2 * LENGTH
    k = np.arange(OUTER)[:, None] + 0.5
    outer_angle = 2 * np.pi * k * np.arange(OUTER)[None] / (2 * OUTER)
    outer = np.concatenate([np.cos(outer_angle), -np.sin(outer_angle)], axis=0)
    m = np.arange(INNER)
    inner_angle = 2 * np.pi * ((m[:, None] * m[None]) % INNER) / INNER
    c, s = np.cos(inner_angle), np.sin(inner_angle)
    inner = np.block([[c, -s], [s, c]])
    twist = 2 * np.pi * k * m[None] / window
    twists = np.stack([np.cos(twist), np.sin(twist)]).astype(np.float32)
    return split(outer), split(outer.T * (2.0 / window)), split(inner), split(inner.T), twists


FAR_FIRST = (2, 1, 3, 0)


class Neighbours:
    def __init__(self, seq, chan):
        self.sy, self.sz, self.sx = lax.div(seq, 8), lax.rem(lax.div(seq, 4), 2), lax.rem(seq, 4)
        self.sz_high, self.core = lax.div(chan, 2), lax.rem(chan, 2)
        self.x = [lax.rem(self.sx + step, 4) for step in range(4)]
        self.y = [lax.rem(self.sy + step, 4) * 8 for step in range(4)]
        self.z_low = [lax.rem(self.sz + step, 2) * 4 for step in range(2)]

    def layer(self, step):
        z = lax.rem(self.sz_high * 2 + self.sz + lax.rem(step, 4), 4)
        core = lax.rem(self.core + lax.div(step, 4), 2)
        return lax.rem(z, 2) * 4, lax.div(z, 2) * 2 + core

    def each_other(self, visit):
        def around(step, own):
            low, chan = self.layer(step)
            for dy in FAR_FIRST:
                for dx in FAR_FIRST:
                    if not (own and dx == 0 and dy == 0):
                        visit(self.y[dy] + low + self.x[dx], chan)

        def body(step, carry):
            around(step, False)
            return carry

        lax.fori_loop(1, 8, body, 0)
        around(0, True)

    def each_in_shard(self, visit):
        for low in (1, 0):
            for dy in FAR_FIRST:
                for dx in FAR_FIRST:
                    visit(self.y[dy] + self.z_low[low] + self.x[dx], low == 0 and dx == 0 and dy == 0)


def route(comp_ref, seq, chan, perm_ref):
    comp = comp_ref[...]
    every = lax.broadcasted_iota(jnp.int32, (1, ALL_CHANNELS), 1)
    low, high = jnp.minimum(comp, every), jnp.maximum(comp, every)
    kind = lax.div(low, CHANNELS) * SHARDS + lax.div(high, CHANNELS)
    kind = jnp.where(every < comp, kind, -1)
    kinds = lax.broadcasted_iota(jnp.int32, (16, ALL_CHANNELS), 0)
    hot = jnp.where(kinds == kind, 1.0, 0.0).astype(BF16)
    start = pl.multiple_of(chan * CHANNELS, CHANNELS)
    own_comp = comp_ref[:, pl.ds(start, CHANNELS)]
    own = lax.broadcasted_iota(jnp.int32, (1, CHANNELS), 1) + start
    own_low, own_high = jnp.minimum(own_comp, own), jnp.maximum(own_comp, own)
    own_first = own < own_comp
    own_kind = lax.div(own_low, CHANNELS) * SHARDS + lax.div(own_high, CHANNELS)
    before = lax.broadcasted_iota(jnp.int32, (ALL_CHANNELS, CHANNELS), 0) < own_low
    before = jnp.where(before, 1.0, 0.0).astype(BF16)
    ranks = jnp.dot(hot, before, preferred_element_type=F32)
    own_kinds = lax.broadcasted_iota(jnp.int32, (16, CHANNELS), 0) == own_kind
    rank = jnp.sum(jnp.where(own_kinds, ranks, 0.0), axis=0, keepdims=True)
    totals = jnp.dot(hot, jnp.ones((ALL_CHANNELS, CHANNELS), BF16), preferred_element_type=F32)
    rank = rank.astype(jnp.int32)
    totals = totals.astype(jnp.int32)
    left = {edge: totals[edge[0] * SHARDS + edge[1]][None] for edge in sorted({e for f in FACTORS for e in f[0]})}
    taken = {edge: jnp.zeros((1, CHANNELS), jnp.int32) for edge in left}
    begin = jnp.zeros((1, CHANNELS), jnp.int32)
    me = chan * SEQ_DEVICES + seq
    place = jnp.zeros((1, CHANNELS), jnp.int32)
    code = jnp.zeros((1, CHANNELS), jnp.int32)
    for chosen, ends, partner in FACTORS:
        count = None
        for edge in sorted(set(chosen)):
            possible = left[edge] if chosen.count(edge) == 1 else lax.shift_right_logical(left[edge], 1)
            count = possible if count is None else jnp.minimum(count, possible)
        for edge in sorted(set(chosen)):
            times = chosen.count(edge)
            first, second = ends[chosen.index(edge)]
            offset = rank - taken[edge]
            size = count * times
            here = (own_kind == edge[0] * SHARDS + edge[1]) & (offset >= 0) & (offset < size)
            if times == 2:
                spot = 2 * begin + offset
            else:
                spot = 2 * (begin + offset) + jnp.where(own_first, first, second)
            place = jnp.where(here, spot, place)
            left[edge] = left[edge] - size
            taken[edge] = taken[edge] + size
        mine = (begin <= me) & (me < begin + count)
        code = jnp.where(mine, sum(p << (3 * i) for i, p in enumerate(partner)), code)
        begin = begin + count
    slots = lax.broadcasted_iota(jnp.int32, (CHANNELS, CHANNELS), 0)
    perm_ref[...] = jnp.where(slots == place, 1.0, 0.0).astype(BF16)
    return jnp.max(code)


def kernel(
    ids_hbm, emb_hbm, gate_hbm, filt_hbm, comp_hbm, grad_hbm,
    outer_hbm, outer_back_hbm, inner_hbm, inner_back_hbm, twist_hbm,
    gate_out, filt_out,
    ids, emb, gate, filt, comp, grad,
    outer, outer_back, inner, inner_back, twist,
    perm, strided, letters, embedded, spectra_k, spectra_g, spectra_u,
    send_k, send_g, send_u, recv_k, recv_g, recv_u,
    send_du, send_dk, recv_du, recv_dk, gate_vmem, filt_vmem,
    load_sem, store_sem, local_sem, send_sem, recv_sem,
):
    spectra = (spectra_k, spectra_g, spectra_u)
    seq, chan = lax.axis_index("seq"), lax.axis_index("chan")
    me = chan * SEQ_DEVICES + seq
    loads = {}
    sources = [
        (comp_hbm, comp), (ids_hbm, ids), (emb_hbm, emb), (filt_hbm, filt), (grad_hbm, grad), (gate_hbm, gate),
        (outer_hbm, outer), (twist_hbm, twist), (inner_hbm, inner), (inner_back_hbm, inner_back),
        (outer_back_hbm, outer_back),
    ]
    for index, (source, target) in enumerate(sources):
        loads[index] = pltpu.make_async_copy(source, target, load_sem.at[index])
        loads[index].start()

    barrier = pltpu.get_barrier_semaphore()

    near = Neighbours(seq, chan)
    near.each_other(
        lambda seq2, chan2: pl.semaphore_signal(barrier, inc=1, device_id=(seq2, chan2), device_id_type=MESH)
    )

    loads[0].wait()
    code = route(comp, seq, chan, perm)

    def lay_out(source_of, target):
        for a in range(ROWS):
            strided[pl.ds(a, CHANNELS, stride=ROWS), :] = source_of(a)
        target[...] = strided[...].reshape(DEVICES, HALF, LANES).astype(BF16)

    def turned(ref):
        def part(a):
            block = ref[pl.ds(a * LANES, LANES), :]
            return lax.dot_general(perm[...], block, (((1,), (1,)), ((), ())), preferred_element_type=F32)
        return part

    def post(source, target, index):
        pltpu.make_async_copy(source.at[me], target.at[me], local_sem.at[index]).start()

        def one(seq2, chan2):
            pltpu.make_async_remote_copy(
                source.at[chan2 * SEQ_DEVICES + seq2], target.at[me], send_sem.at[index], recv_sem.at[index],
                device_id=(seq2, chan2), device_id_type=MESH,
            ).start()

        near.each_other(one)

    def arrived(source, target, index):
        pltpu.make_async_copy(source.at[me], target.at[me], local_sem.at[index]).wait()
        rest = pl.ds(0, DEVICES - 1)
        pltpu.make_async_copy(target.at[rest], target.at[rest], recv_sem.at[index]).wait()

    def left_here(source, index):
        rest = pl.ds(0, DEVICES - 1)
        pltpu.make_async_copy(source.at[rest], source.at[rest], send_sem.at[index]).wait()

    loads[3].wait()
    lay_out(turned(filt), send_k)
    pl.semaphore_wait(barrier, DEVICES - 1)
    post(send_k, recv_k, 0)

    loads[4].wait()
    lay_out(turned(grad), send_g)
    post(send_g, recv_g, 1)

    loads[1].wait()
    loads[2].wait()
    names = lax.broadcasted_iota(jnp.int32, (4, ALL_CHANNELS), 0)
    letters[...] = jnp.where(names == ids[...], 1.0, 0.0).astype(BF16)
    own_emb = lax.dot_general(perm[...], emb[...], (((1,), (1,)), ((), ())), preferred_element_type=F32).astype(BF16)
    for a in range(ROWS):
        embedded[a] = jnp.dot(own_emb, letters[:, a * LANES : (a + 1) * LANES], preferred_element_type=F32)
    loads[5].wait()
    turn_gate = turned(gate)
    lay_out(lambda a: turn_gate(a) * embedded[a], send_u)
    post(send_u, recv_u, 2)

    for index in range(6, 11):
        loads[index].wait()

    def times(matrices, right):
        return jnp.dot(matrices[0], right, preferred_element_type=F32) + jnp.dot(
            matrices[1], right, preferred_element_type=F32
        )

    def times_right(left, matrices):
        return jnp.dot(left, matrices[0], preferred_element_type=F32) + jnp.dot(
            left, matrices[1], preferred_element_type=F32
        )

    def forward(received, shard):
        block = received[pl.ds(shard * SEQ_DEVICES, SEQ_DEVICES)].astype(F32)
        block = block.reshape(SEQ_DEVICES, 2, ROWS, LANES)
        fields = [block[:, slot].reshape(OUTER, INNER) for slot in range(2)]
        mixed = times(outer, jnp.concatenate(fields, axis=1).astype(BF16))
        cos, sin = twist[0], twist[1]
        spread = []
        for slot in range(2):
            real = mixed[:OUTER, slot * INNER : (slot + 1) * INNER]
            imag = mixed[OUTER:, slot * INNER : (slot + 1) * INNER]
            spread.append(jnp.concatenate([real * cos + imag * sin, imag * cos - real * sin], axis=1))
        return times_right(jnp.concatenate(spread, axis=0).astype(BF16), inner)

    def backward(parts):
        rows = [jnp.concatenate([real, imag], axis=1) for real, imag in parts]
        mixed = times_right(jnp.concatenate(rows, axis=0).astype(BF16), inner_back)
        cos, sin = twist[0], twist[1]
        spread = []
        for slot in range(2):
            real = mixed[slot * OUTER : (slot + 1) * OUTER, :INNER]
            imag = mixed[slot * OUTER : (slot + 1) * OUTER, INNER:]
            spread.append(jnp.concatenate([real * cos - imag * sin, imag * cos + real * sin], axis=0))
        fields = times(outer_back, jnp.concatenate(spread, axis=1).astype(BF16))
        halves = [
            fields[:, slot * INNER : (slot + 1) * INNER].reshape(SEQ_DEVICES, 1, ROWS, LANES) for slot in range(2)
        ]
        return jnp.concatenate(halves, axis=1).reshape(SEQ_DEVICES, HALF, LANES).astype(BF16)

    def spectrum(kind, channel):
        both = spectra[kind][channel]
        return both[:, :INNER], both[:, INNER:]

    def partner_of(channel):
        return lax.rem(lax.shift_right_logical(code, 3 * channel), SHARE)

    def forward_shard(received, kind, finish, shard):
        both = forward(received, shard)
        for slot in range(2):
            channel = 2 * shard + slot
            spectra[kind][channel] = finish(both[slot * OUTER : (slot + 1) * OUTER], channel)

    def all_forward(received, kind, finish):
        def body(shard, carry):
            forward_shard(received, kind, finish, shard)
            return carry

        lax.fori_loop(0, SHARDS, body, 0, unroll=UNROLL)

    def all_backward(prepare, combine, source, target, index):
        def body(turn, carry):
            shard = lax.rem(chan + 1 + turn, SHARDS)
            base = shard * SEQ_DEVICES
            prepare(shard)
            source[pl.ds(base, SEQ_DEVICES)] = backward([combine(2 * shard + slot) for slot in range(2)])

            def one(seq2, own):
                def other():
                    pltpu.make_async_remote_copy(
                        source.at[base + seq2], target.at[me], send_sem.at[index], recv_sem.at[index],
                        device_id=(seq2, shard), device_id_type=MESH,
                    ).start()

                if own:
                    pl.when(turn < SHARDS - 1)(other)
                else:
                    other()

            near.each_in_shard(one)
            return carry

        lax.fori_loop(0, SHARDS, body, 0, unroll=UNROLL)
        pltpu.make_async_copy(source.at[me], target.at[me], local_sem.at[index]).start()

    arrived(send_k, recv_k, 0)
    all_forward(recv_k, 0, lambda both, channel: both)
    arrived(send_g, recv_g, 1)

    def input_spectrum(channel):
        k_real, k_imag = spectrum(0, channel)
        p_real, p_imag = spectrum(0, partner_of(channel))
        g_real, g_imag = spectrum(1, channel)
        real, imag = k_real + p_real, p_imag - k_imag
        return g_real * real - g_imag * imag, g_real * imag + g_imag * real

    all_forward(recv_g, 1, lambda both, channel: both)
    all_backward(lambda shard: None, input_spectrum, send_du, recv_du, 3)

    def product(both, channel):
        g_real, g_imag = spectrum(1, channel)
        u_real, u_imag = both[:, :INNER], both[:, INNER:]
        return jnp.concatenate([g_real * u_real + g_imag * u_imag, g_imag * u_real - g_real * u_imag], axis=1)

    arrived(send_u, recv_u, 2)
    all_forward(recv_u, 2, product)

    def filter_spectrum(channel):
        real, imag = spectrum(2, channel)
        p_real, p_imag = spectrum(2, partner_of(channel))
        return real + p_real, imag - p_imag

    all_backward(lambda shard: None, filter_spectrum, send_dk, recv_dk, 4)

    def give_back(received, scale, target):
        strided[...] = received[...].astype(F32).reshape(DEVICES * HALF, LANES)
        for a in range(ROWS):
            part = scale(strided[pl.ds(a, CHANNELS, stride=ROWS), :], a).astype(BF16)
            block = lax.dot_general(part, perm[...], (((0,), (0,)), ((), ())), preferred_element_type=F32)
            target[pl.ds(a * LANES, LANES), :] = block.astype(target.dtype)

    arrived(send_du, recv_du, 3)
    give_back(recv_du, lambda part, a: part * embedded[a], gate_vmem)
    gate_store = pltpu.make_async_copy(gate_vmem, gate_out, store_sem.at[0])
    gate_store.start()
    arrived(send_dk, recv_dk, 4)
    give_back(recv_dk, lambda part, a: part, filt_vmem)
    filt_store = pltpu.make_async_copy(filt_vmem, filt_out, store_sem.at[1])
    filt_store.start()
    for index, source in enumerate([send_k, send_g, send_u, send_du, send_dk]):
        left_here(source, index)
    gate_store.wait()
    filt_store.wait()


def shards(base_ids, embedding, gate_values, filter_kernel, complement, output_gradient):
    positions, channels = filter_kernel.shape
    tables = transform_tables()
    blocks = pltpu.VMEM((DEVICES, HALF, LANES), BF16)
    gate_gradient, filter_gradient = pl.pallas_call(
        kernel,
        out_shape=[
            jax.ShapeDtypeStruct((positions, channels), BF16),
            jax.ShapeDtypeStruct((positions, channels), BF16),
        ],
        in_specs=[pl.BlockSpec(memory_space=pl.ANY)] * 11,
        out_specs=[pl.BlockSpec(memory_space=pl.ANY)] * 2,
        scratch_shapes=[
            pltpu.VMEM((1, positions), jnp.int32),
            pltpu.VMEM(embedding.shape, BF16),
            pltpu.VMEM((positions, channels), BF16),
            pltpu.VMEM((positions, channels), BF16),
            pltpu.VMEM((1, ALL_CHANNELS), jnp.int32),
            pltpu.VMEM((positions, channels), BF16),
            *[pltpu.VMEM(table.shape, table.dtype) for table in tables],
            pltpu.VMEM((channels, channels), BF16),
            pltpu.VMEM((DEVICES * HALF, LANES), F32),
            pltpu.VMEM((4, positions), BF16),
            pltpu.VMEM((ROWS, channels, LANES), F32),
            *[pltpu.VMEM((SHARE, OUTER, 2 * INNER), F32)] * 3,
            *[blocks] * 10,
            pltpu.VMEM((positions, channels), BF16),
            pltpu.VMEM((positions, channels), BF16),
            pltpu.SemaphoreType.DMA((11,)),
            pltpu.SemaphoreType.DMA((2,)),
            pltpu.SemaphoreType.DMA((5,)),
            pltpu.SemaphoreType.DMA((5,)),
            pltpu.SemaphoreType.DMA((5,)),
        ],
        compiler_params=pltpu.CompilerParams(collective_id=0, has_side_effects=True, vmem_limit_bytes=62 << 20),
        name="two_strand_gradients",
    )(
        base_ids, embedding, gate_values.reshape(positions, channels), filter_kernel,
        complement.reshape(1, -1), output_gradient.reshape(positions, channels),
        *[jnp.asarray(table) for table in tables],
    )
    return gate_gradient[None], filter_gradient.astype(F32)


def solution(mesh):
    in_specs = (
        P(None, "seq"),
        P(None, "chan"),
        P(None, "seq", "chan"),
        P("seq", "chan"),
        P(),
        P(None, "seq", "chan"),
    )
    out_specs = (P(None, "seq", "chan"), P("seq", "chan"))
    return jax.shard_map(shards, mesh=mesh, in_specs=in_specs, out_specs=out_specs, check_vma=False)
```

```python
import functools
import itertools
import math

import jax
import jax.numpy as jnp
import numpy as np
from jax import lax
from jax.experimental import pallas as pl
from jax.experimental.pallas import tpu as pltpu
from jax.sharding import PartitionSpec as P

MESH = pl.DeviceIdType.MESH
F32 = jnp.float32
BF16 = jnp.bfloat16
SHARDS = 4
SEQ_DEVICES = 32
DEVICES = SHARDS * SEQ_DEVICES
LANES = 128
ROWS = 8
LENGTH = 32768
SHARE = 2 * SHARDS
INNER = 128
OUTER = LENGTH // INNER
HALF = 2 * ROWS
CHANNELS = 256
ALL_CHANNELS = SHARDS * CHANNELS
UNROLL = 4


def two_factors():
    edges = [(a, b) for a in range(SHARDS) for b in range(a, SHARDS)]
    found = []
    for chosen in itertools.combinations_with_replacement(edges, SHARDS):
        degrees = [sum(edge.count(shard) for edge in chosen) for shard in range(SHARDS)]
        if degrees == [2] * SHARDS:
            found.append(chosen)
    return found


def slots_of(chosen):
    used = [0] * SHARDS
    ends = []
    partner = [0] * SHARE
    for a, b in chosen:
        first = used[a]
        used[a] += 1
        second = used[b]
        used[b] += 1
        ends.append((first, second))
        partner[2 * a + first] = 2 * b + second
        partner[2 * b + second] = 2 * a + first
    return ends, partner


FACTORS = [(chosen, *slots_of(chosen)) for chosen in two_factors()]


def split(table):
    high = table.astype(np.float32).astype(jnp.bfloat16)
    low = (table.astype(np.float32) - high.astype(np.float32)).astype(jnp.bfloat16)
    return np.stack([high, low])


def transform_tables():
    window = 2 * LENGTH
    k = np.arange(OUTER)[:, None] + 0.5
    outer_angle = 2 * np.pi * k * np.arange(OUTER)[None] / (2 * OUTER)
    outer = np.concatenate([np.cos(outer_angle), -np.sin(outer_angle)], axis=0)
    m = np.arange(INNER)
    inner_angle = 2 * np.pi * ((m[:, None] * m[None]) % INNER) / INNER
    c, s = np.cos(inner_angle), np.sin(inner_angle)
    inner = np.block([[c, -s], [s, c]])
    twist = 2 * np.pi * k * m[None] / window
    twists = np.stack([np.cos(twist), np.sin(twist)]).astype(np.float32)
    return split(outer), split(outer.T * (2.0 / window)), split(inner), split(inner.T), twists


FAR_FIRST = (2, 1, 3, 0)


class Neighbours:
    def __init__(self, seq, chan):
        self.sy, self.sz, self.sx = lax.div(seq, 8), lax.rem(lax.div(seq, 4), 2), lax.rem(seq, 4)
        self.sz_high, self.core = lax.div(chan, 2), lax.rem(chan, 2)
        self.x = [lax.rem(self.sx + step, 4) for step in range(4)]
        self.y = [lax.rem(self.sy + step, 4) * 8 for step in range(4)]

    def layer(self, step):
        z = lax.rem(self.sz_high * 2 + self.sz + lax.rem(step, 4), 4)
        core = lax.rem(self.core + lax.div(step, 4), 2)
        return lax.rem(z, 2) * 4, lax.div(z, 2) * 2 + core

    def each_other(self, visit):
        def around(step, own):
            low, chan = self.layer(step)
            for dy in FAR_FIRST:
                for dx in FAR_FIRST:
                    if not (own and dx == 0 and dy == 0):
                        visit(self.y[dy] + low + self.x[dx], chan)

        def body(step, carry):
            around(step, False)
            return carry

        lax.fori_loop(1, 8, body, 0)
        around(0, True)


def route(comp_ref, seq, chan, perm_ref):
    comp = comp_ref[...]
    every = lax.broadcasted_iota(jnp.int32, (1, ALL_CHANNELS), 1)
    low, high = jnp.minimum(comp, every), jnp.maximum(comp, every)
    kind = lax.div(low, CHANNELS) * SHARDS + lax.div(high, CHANNELS)
    kind = jnp.where(every < comp, kind, -1)
    kinds = lax.broadcasted_iota(jnp.int32, (16, ALL_CHANNELS), 0)
    hot = jnp.where(kinds == kind, 1.0, 0.0).astype(BF16)
    start = pl.multiple_of(chan * CHANNELS, CHANNELS)
    own_comp = comp_ref[:, pl.ds(start, CHANNELS)]
    own = lax.broadcasted_iota(jnp.int32, (1, CHANNELS), 1) + start
    own_low, own_high = jnp.minimum(own_comp, own), jnp.maximum(own_comp, own)
    own_first = own < own_comp
    own_kind = lax.div(own_low, CHANNELS) * SHARDS + lax.div(own_high, CHANNELS)
    before = lax.broadcasted_iota(jnp.int32, (ALL_CHANNELS, CHANNELS), 0) < own_low
    before = jnp.where(before, 1.0, 0.0).astype(BF16)
    ranks = jnp.dot(hot, before, preferred_element_type=F32)
    own_kinds = lax.broadcasted_iota(jnp.int32, (16, CHANNELS), 0) == own_kind
    rank = jnp.sum(jnp.where(own_kinds, ranks, 0.0), axis=0, keepdims=True)
    totals = jnp.dot(hot, jnp.ones((ALL_CHANNELS, CHANNELS), BF16), preferred_element_type=F32)
    rank = rank.astype(jnp.int32)
    totals = totals.astype(jnp.int32)
    left = {edge: totals[edge[0] * SHARDS + edge[1]][None] for edge in sorted({e for f in FACTORS for e in f[0]})}
    taken = {edge: jnp.zeros((1, CHANNELS), jnp.int32) for edge in left}
    begin = jnp.zeros((1, CHANNELS), jnp.int32)
    me = chan * SEQ_DEVICES + seq
    place = jnp.zeros((1, CHANNELS), jnp.int32)
    code = jnp.zeros((1, CHANNELS), jnp.int32)
    for chosen, ends, partner in FACTORS:
        count = None
        for edge in sorted(set(chosen)):
            possible = left[edge] if chosen.count(edge) == 1 else lax.shift_right_logical(left[edge], 1)
            count = possible if count is None else jnp.minimum(count, possible)
        for edge in sorted(set(chosen)):
            times = chosen.count(edge)
            first, second = ends[chosen.index(edge)]
            offset = rank - taken[edge]
            size = count * times
            here = (own_kind == edge[0] * SHARDS + edge[1]) & (offset >= 0) & (offset < size)
            if times == 2:
                spot = 2 * begin + offset
            else:
                spot = 2 * (begin + offset) + jnp.where(own_first, first, second)
            place = jnp.where(here, spot, place)
            left[edge] = left[edge] - size
            taken[edge] = taken[edge] + size
        mine = (begin <= me) & (me < begin + count)
        code = jnp.where(mine, sum(p << (3 * i) for i, p in enumerate(partner)), code)
        begin = begin + count
    slots = lax.broadcasted_iota(jnp.int32, (CHANNELS, CHANNELS), 0)
    perm_ref[...] = jnp.where(slots == place, 1.0, 0.0).astype(BF16)
    return jnp.max(code)


def put_back(part, perm):
    return lax.dot_general(part, perm[...], (((0,), (0,)), ((), ())), preferred_element_type=F32)


def kernel(
    ids_hbm, emb_hbm, gate_hbm, filt_hbm, comp_hbm, grad_hbm,
    outer_hbm, outer_back_hbm, inner_hbm, inner_back_hbm, twist_hbm,
    gate_out, recv_dk, perm_out,
    ids, emb, gate, filt, comp, grad,
    outer, outer_back, inner, inner_back, twist,
    perm, strided, letters, embedded, spectra_k, spectra_g, spectra_u,
    send_k, send_g, send_u, recv_k, recv_g, recv_u,
    send_du, send_dk, recv_du, gate_vmem,
    load_sem, store_sem, local_sem, send_sem, recv_sem,
):
    spectra = (spectra_k, spectra_g, spectra_u)
    seq, chan = lax.axis_index("seq"), lax.axis_index("chan")
    me = chan * SEQ_DEVICES + seq
    loads = {}
    sources = [
        (comp_hbm, comp), (ids_hbm, ids), (emb_hbm, emb), (filt_hbm, filt), (grad_hbm, grad), (gate_hbm, gate),
        (outer_hbm, outer), (twist_hbm, twist), (inner_hbm, inner), (inner_back_hbm, inner_back),
        (outer_back_hbm, outer_back),
    ]
    for index, (source, target) in enumerate(sources):
        loads[index] = pltpu.make_async_copy(source, target, load_sem.at[index])
        loads[index].start()

    barrier = pltpu.get_barrier_semaphore()

    near = Neighbours(seq, chan)
    near.each_other(
        lambda seq2, chan2: pl.semaphore_signal(barrier, inc=1, device_id=(seq2, chan2), device_id_type=MESH)
    )

    loads[0].wait()
    code = route(comp, seq, chan, perm)
    perm_store = pltpu.make_async_copy(perm, perm_out, store_sem.at[1])
    perm_store.start()

    def lay_out(source_of, target):
        for a in range(ROWS):
            strided[pl.ds(a, CHANNELS, stride=ROWS), :] = source_of(a)
        target[...] = strided[...].reshape(DEVICES, HALF, LANES).astype(BF16)

    def turned(ref):
        def part(a):
            block = ref[pl.ds(a * LANES, LANES), :]
            return lax.dot_general(perm[...], block, (((1,), (1,)), ((), ())), preferred_element_type=F32)
        return part

    def post(source, target, index):
        pltpu.make_async_copy(source.at[me], target.at[me], local_sem.at[index]).start()

        def one(seq2, chan2):
            pltpu.make_async_remote_copy(
                source.at[chan2 * SEQ_DEVICES + seq2], target.at[me], send_sem.at[index], recv_sem.at[index],
                device_id=(seq2, chan2), device_id_type=MESH,
            ).start()

        near.each_other(one)

    def arrived(source, target, index):
        pltpu.make_async_copy(source.at[me], target.at[me], local_sem.at[index]).wait()
        rest = pl.ds(0, DEVICES - 1)
        pltpu.make_async_copy(target.at[rest], target.at[rest], recv_sem.at[index]).wait()

    def left_here(source, index):
        rest = pl.ds(0, DEVICES - 1)
        pltpu.make_async_copy(source.at[rest], source.at[rest], send_sem.at[index]).wait()

    loads[3].wait()
    lay_out(turned(filt), send_k)
    pl.semaphore_wait(barrier, DEVICES - 1)
    post(send_k, recv_k, 0)

    loads[4].wait()
    lay_out(turned(grad), send_g)
    post(send_g, recv_g, 1)

    loads[1].wait()
    loads[2].wait()
    names = lax.broadcasted_iota(jnp.int32, (4, ALL_CHANNELS), 0)
    letters[...] = jnp.where(names == ids[...], 1.0, 0.0).astype(BF16)
    own_emb = lax.dot_general(perm[...], emb[...], (((1,), (1,)), ((), ())), preferred_element_type=F32).astype(BF16)
    for a in range(ROWS):
        embedded[a] = jnp.dot(own_emb, letters[:, a * LANES : (a + 1) * LANES], preferred_element_type=F32)
    loads[5].wait()
    turn_gate = turned(gate)
    lay_out(lambda a: turn_gate(a) * embedded[a], send_u)

    for index in range(6, 11):
        loads[index].wait()

    def times(matrices, right):
        return jnp.dot(matrices[0], right, preferred_element_type=F32) + jnp.dot(
            matrices[1], right, preferred_element_type=F32
        )

    def times_right(left, matrices):
        return jnp.dot(left, matrices[0], preferred_element_type=F32) + jnp.dot(
            left, matrices[1], preferred_element_type=F32
        )

    def forward(received, shard):
        block = received[pl.ds(shard * SEQ_DEVICES, SEQ_DEVICES)].astype(F32)
        block = block.reshape(SEQ_DEVICES, 2, ROWS, LANES)
        fields = [block[:, slot].reshape(OUTER, INNER) for slot in range(2)]
        mixed = times(outer, jnp.concatenate(fields, axis=1).astype(BF16))
        cos, sin = twist[0], twist[1]
        spread = []
        for slot in range(2):
            real = mixed[:OUTER, slot * INNER : (slot + 1) * INNER]
            imag = mixed[OUTER:, slot * INNER : (slot + 1) * INNER]
            spread.append(jnp.concatenate([real * cos + imag * sin, imag * cos - real * sin], axis=1))
        return times_right(jnp.concatenate(spread, axis=0).astype(BF16), inner)

    def backward(parts):
        rows = [jnp.concatenate([real, imag], axis=1) for real, imag in parts]
        mixed = times_right(jnp.concatenate(rows, axis=0).astype(BF16), inner_back)
        cos, sin = twist[0], twist[1]
        spread = []
        for slot in range(2):
            real = mixed[slot * OUTER : (slot + 1) * OUTER, :INNER]
            imag = mixed[slot * OUTER : (slot + 1) * OUTER, INNER:]
            spread.append(jnp.concatenate([real * cos - imag * sin, imag * cos + real * sin], axis=0))
        fields = times(outer_back, jnp.concatenate(spread, axis=1).astype(BF16))
        halves = [
            fields[:, slot * INNER : (slot + 1) * INNER].reshape(SEQ_DEVICES, 1, ROWS, LANES) for slot in range(2)
        ]
        return jnp.concatenate(halves, axis=1).reshape(SEQ_DEVICES, HALF, LANES).astype(BF16)

    def spectrum(kind, channel):
        both = spectra[kind][channel]
        return both[:, :INNER], both[:, INNER:]

    def partner_of(channel):
        return lax.rem(lax.shift_right_logical(code, 3 * channel), SHARE)

    def forward_shard(received, kind, finish, shard):
        both = forward(received, shard)
        for slot in range(2):
            channel = 2 * shard + slot
            spectra[kind][channel] = finish(both[slot * OUTER : (slot + 1) * OUTER], channel)

    def all_forward(received, kind, finish):
        def body(shard, carry):
            forward_shard(received, kind, finish, shard)
            return carry

        lax.fori_loop(0, SHARDS, body, 0, unroll=UNROLL)

    def all_backward(combine, source):
        def body(shard, carry):
            source[pl.ds(shard * SEQ_DEVICES, SEQ_DEVICES)] = backward([combine(2 * shard + slot) for slot in range(2)])
            return carry

        lax.fori_loop(0, SHARDS, body, 0, unroll=UNROLL)

    arrived(send_k, recv_k, 0)
    post(send_u, recv_u, 2)
    all_forward(recv_k, 0, lambda both, channel: both)
    arrived(send_g, recv_g, 1)

    def input_spectrum(channel):
        k_real, k_imag = spectrum(0, channel)
        p_real, p_imag = spectrum(0, partner_of(channel))
        g_real, g_imag = spectrum(1, channel)
        real, imag = k_real + p_real, p_imag - k_imag
        return g_real * real - g_imag * imag, g_real * imag + g_imag * real

    all_forward(recv_g, 1, lambda both, channel: both)
    all_backward(input_spectrum, send_du)
    post(send_du, recv_du, 3)

    def product(both, channel):
        g_real, g_imag = spectrum(1, channel)
        u_real, u_imag = both[:, :INNER], both[:, INNER:]
        return jnp.concatenate([g_real * u_real + g_imag * u_imag, g_imag * u_real - g_real * u_imag], axis=1)

    arrived(send_u, recv_u, 2)
    all_forward(recv_u, 2, product)

    def filter_spectrum(channel):
        real, imag = spectrum(2, channel)
        p_real, p_imag = spectrum(2, partner_of(channel))
        return real + p_real, imag - p_imag

    all_backward(filter_spectrum, send_dk)
    post(send_dk, recv_dk, 4)

    arrived(send_du, recv_du, 3)
    strided[...] = recv_du[...].astype(F32).reshape(DEVICES * HALF, LANES)
    for a in range(ROWS):
        part = (strided[pl.ds(a, CHANNELS, stride=ROWS), :] * embedded[a]).astype(BF16)
        gate_vmem[pl.ds(a * LANES, LANES), :] = put_back(part, perm).astype(BF16)
    gate_store = pltpu.make_async_copy(gate_vmem, gate_out, store_sem.at[0])
    gate_store.start()
    arrived(send_dk, recv_dk, 4)
    for index, source in enumerate([send_k, send_g, send_u, send_du, send_dk]):
        left_here(source, index)
    gate_store.wait()
    perm_store.wait()


def finish(gate_hbm, back_hbm, perm_hbm, gate_out, filt_out, gate, back, perm, strided, filt, load_sem, store_sem):
    gate_load = pltpu.make_async_copy(gate_hbm, gate, load_sem.at[2])
    gate_store = pltpu.make_async_copy(gate, gate_out, store_sem.at[ROWS])
    back_load = pltpu.make_async_copy(back_hbm, back, load_sem.at[0])
    perm_load = pltpu.make_async_copy(perm_hbm, perm, load_sem.at[1])
    back_load.start()
    perm_load.start()
    gate_load.start()
    back_load.wait()
    strided[...] = back[...].astype(F32).reshape(DEVICES * HALF, LANES)
    gate_load.wait()
    gate_store.start()
    perm_load.wait()
    stores = []
    for a in range(ROWS):
        part = strided[pl.ds(a, CHANNELS, stride=ROWS), :].astype(BF16)
        rows = pl.ds(a * LANES, LANES)
        filt[rows, :] = put_back(part, perm)
        stores.append(pltpu.make_async_copy(filt.at[rows], filt_out.at[rows], store_sem.at[a]))
        stores[-1].start()
    for store in stores:
        store.wait()
    gate_store.wait()


def shards(base_ids, embedding, gate_values, filter_kernel, complement, output_gradient):
    positions, channels = filter_kernel.shape
    tables = transform_tables()
    blocks = pltpu.VMEM((DEVICES, HALF, LANES), BF16)
    parts = pl.pallas_call(
        kernel,
        out_shape=[
            jax.ShapeDtypeStruct((positions, channels), BF16),
            jax.ShapeDtypeStruct((DEVICES, HALF, LANES), BF16),
            jax.ShapeDtypeStruct((channels, channels), BF16),
        ],
        in_specs=[pl.BlockSpec(memory_space=pl.ANY)] * 11,
        out_specs=[pl.BlockSpec(memory_space=pl.ANY)] * 3,
        scratch_shapes=[
            pltpu.VMEM((1, positions), jnp.int32),
            pltpu.VMEM(embedding.shape, BF16),
            pltpu.VMEM((positions, channels), BF16),
            pltpu.VMEM((positions, channels), BF16),
            pltpu.VMEM((1, ALL_CHANNELS), jnp.int32),
            pltpu.VMEM((positions, channels), BF16),
            *[pltpu.VMEM(table.shape, table.dtype) for table in tables],
            pltpu.VMEM((channels, channels), BF16),
            pltpu.VMEM((DEVICES * HALF, LANES), F32),
            pltpu.VMEM((4, positions), BF16),
            pltpu.VMEM((ROWS, channels, LANES), F32),
            *[pltpu.VMEM((SHARE, OUTER, 2 * INNER), F32)] * 3,
            *[blocks] * 9,
            pltpu.VMEM((positions, channels), BF16),
            pltpu.SemaphoreType.DMA((11,)),
            pltpu.SemaphoreType.DMA((2,)),
            pltpu.SemaphoreType.DMA((5,)),
            pltpu.SemaphoreType.DMA((5,)),
            pltpu.SemaphoreType.DMA((5,)),
        ],
        compiler_params=pltpu.CompilerParams(collective_id=0, has_side_effects=True, vmem_limit_bytes=62 << 20),
        name="two_strand_gradients",
    )(
        base_ids, embedding, gate_values.reshape(positions, channels), filter_kernel,
        complement.reshape(1, -1), output_gradient.reshape(positions, channels),
        *[jnp.asarray(table) for table in tables],
    )
    gate_gradient, filter_gradient = pl.pallas_call(
        finish,
        out_shape=[
            jax.ShapeDtypeStruct((positions, channels), BF16),
            jax.ShapeDtypeStruct((positions, channels), F32),
        ],
        in_specs=[pl.BlockSpec(memory_space=pl.ANY)] * 3,
        out_specs=[pl.BlockSpec(memory_space=pl.ANY)] * 2,
        scratch_shapes=[
            pltpu.VMEM((positions, channels), BF16),
            blocks,
            pltpu.VMEM((channels, channels), BF16),
            pltpu.VMEM((DEVICES * HALF, LANES), F32),
            pltpu.VMEM((positions, channels), F32),
            pltpu.SemaphoreType.DMA((3,)),
            pltpu.SemaphoreType.DMA((ROWS + 1,)),
        ],
        compiler_params=pltpu.CompilerParams(vmem_limit_bytes=62 << 20),
        name="positions_by_channels",
    )(*parts)
    return gate_gradient[None], filter_gradient


def solution(mesh):
    in_specs = (
        P(None, "seq"),
        P(None, "chan"),
        P(None, "seq", "chan"),
        P("seq", "chan"),
        P(),
        P(None, "seq", "chan"),
    )
    out_specs = (P(None, "seq", "chan"), P("seq", "chan"))
    return jax.shard_map(shards, mesh=mesh, in_specs=in_specs, out_specs=out_specs, check_vma=False)
```

```python
import functools
import itertools
import math

import jax
import jax.numpy as jnp
import numpy as np
from jax import lax
from jax.experimental import pallas as pl
from jax.experimental.pallas import tpu as pltpu
from jax.sharding import PartitionSpec as P

MESH = pl.DeviceIdType.MESH
F32 = jnp.float32
BF16 = jnp.bfloat16
SHARDS = 4
SEQ_DEVICES = 32
DEVICES = SHARDS * SEQ_DEVICES
LANES = 128
ROWS = 8
LENGTH = 32768
SHARE = 2 * SHARDS
INNER = 128
OUTER = LENGTH // INNER
HALF = 2 * ROWS
CHANNELS = 256
ALL_CHANNELS = SHARDS * CHANNELS
UNROLL = 4


def two_factors():
    edges = [(a, b) for a in range(SHARDS) for b in range(a, SHARDS)]
    found = []
    for chosen in itertools.combinations_with_replacement(edges, SHARDS):
        degrees = [sum(edge.count(shard) for edge in chosen) for shard in range(SHARDS)]
        if degrees == [2] * SHARDS:
            found.append(chosen)
    return found


def slots_of(chosen):
    used = [0] * SHARDS
    ends = []
    partner = [0] * SHARE
    for a, b in chosen:
        first = used[a]
        used[a] += 1
        second = used[b]
        used[b] += 1
        ends.append((first, second))
        partner[2 * a + first] = 2 * b + second
        partner[2 * b + second] = 2 * a + first
    return ends, partner


FACTORS = [(chosen, *slots_of(chosen)) for chosen in two_factors()]


def split(table):
    high = table.astype(np.float32).astype(jnp.bfloat16)
    low = (table.astype(np.float32) - high.astype(np.float32)).astype(jnp.bfloat16)
    return np.stack([high, low])


def transform_tables():
    window = 2 * LENGTH
    k = np.arange(OUTER)[:, None] + 0.5
    outer_angle = 2 * np.pi * k * np.arange(OUTER)[None] / (2 * OUTER)
    outer = np.concatenate([np.cos(outer_angle), -np.sin(outer_angle)], axis=0)
    m = np.arange(INNER)
    inner_angle = 2 * np.pi * ((m[:, None] * m[None]) % INNER) / INNER
    c, s = np.cos(inner_angle), np.sin(inner_angle)
    inner = np.block([[c, -s], [s, c]])
    twist = 2 * np.pi * k * m[None] / window
    twists = np.stack([np.cos(twist), np.sin(twist)]).astype(np.float32)
    return split(outer), split(outer.T * (2.0 / window)), split(inner), split(inner.T), twists


FAR_FIRST = (2, 1, 3, 0)


class Neighbours:
    def __init__(self, seq, chan):
        self.sy, self.sz, self.sx = lax.div(seq, 8), lax.rem(lax.div(seq, 4), 2), lax.rem(seq, 4)
        self.sz_high, self.core = lax.div(chan, 2), lax.rem(chan, 2)
        self.x = [lax.rem(self.sx + step, 4) for step in range(4)]
        self.y = [lax.rem(self.sy + step, 4) * 8 for step in range(4)]

    def layer(self, step):
        z = lax.rem(self.sz_high * 2 + self.sz + lax.rem(step, 4), 4)
        core = lax.rem(self.core + lax.div(step, 4), 2)
        return lax.rem(z, 2) * 4, lax.div(z, 2) * 2 + core

    def each_in_half(self, other_core, visit):
        def around(step, own):
            low, chan = self.layer(step)
            for dy in FAR_FIRST:
                for dx in FAR_FIRST:
                    if not (own and dx == 0 and dy == 0):
                        visit(self.y[dy] + low + self.x[dx], chan)

        def body(step, carry):
            around(step, False)
            return carry

        if other_core:
            lax.fori_loop(4, 8, body, 0)
        else:
            lax.fori_loop(1, 4, body, 0)
            around(0, True)

    def each_other(self, visit):
        self.each_in_half(1, visit)
        self.each_in_half(0, visit)


def route(comp_ref, seq, chan, perm_ref):
    comp = comp_ref[...]
    every = lax.broadcasted_iota(jnp.int32, (1, ALL_CHANNELS), 1)
    low, high = jnp.minimum(comp, every), jnp.maximum(comp, every)
    kind = lax.div(low, CHANNELS) * SHARDS + lax.div(high, CHANNELS)
    kind = jnp.where(every < comp, kind, -1)
    kinds = lax.broadcasted_iota(jnp.int32, (16, ALL_CHANNELS), 0)
    hot = jnp.where(kinds == kind, 1.0, 0.0).astype(BF16)
    start = pl.multiple_of(chan * CHANNELS, CHANNELS)
    own_comp = comp_ref[:, pl.ds(start, CHANNELS)]
    own = lax.broadcasted_iota(jnp.int32, (1, CHANNELS), 1) + start
    own_low, own_high = jnp.minimum(own_comp, own), jnp.maximum(own_comp, own)
    own_first = own < own_comp
    own_kind = lax.div(own_low, CHANNELS) * SHARDS + lax.div(own_high, CHANNELS)
    before = lax.broadcasted_iota(jnp.int32, (ALL_CHANNELS, CHANNELS), 0) < own_low
    before = jnp.where(before, 1.0, 0.0).astype(BF16)
    ranks = jnp.dot(hot, before, preferred_element_type=F32)
    own_kinds = lax.broadcasted_iota(jnp.int32, (16, CHANNELS), 0) == own_kind
    rank = jnp.sum(jnp.where(own_kinds, ranks, 0.0), axis=0, keepdims=True)
    totals = jnp.dot(hot, jnp.ones((ALL_CHANNELS, CHANNELS), BF16), preferred_element_type=F32)
    rank = rank.astype(jnp.int32)
    totals = totals.astype(jnp.int32)
    left = {edge: totals[edge[0] * SHARDS + edge[1]][None] for edge in sorted({e for f in FACTORS for e in f[0]})}
    taken = {edge: jnp.zeros((1, CHANNELS), jnp.int32) for edge in left}
    begin = jnp.zeros((1, CHANNELS), jnp.int32)
    me = chan * SEQ_DEVICES + seq
    place = jnp.zeros((1, CHANNELS), jnp.int32)
    code = jnp.zeros((1, CHANNELS), jnp.int32)
    for chosen, ends, partner in FACTORS:
        count = None
        for edge in sorted(set(chosen)):
            possible = left[edge] if chosen.count(edge) == 1 else lax.shift_right_logical(left[edge], 1)
            count = possible if count is None else jnp.minimum(count, possible)
        for edge in sorted(set(chosen)):
            times = chosen.count(edge)
            first, second = ends[chosen.index(edge)]
            offset = rank - taken[edge]
            size = count * times
            here = (own_kind == edge[0] * SHARDS + edge[1]) & (offset >= 0) & (offset < size)
            if times == 2:
                spot = 2 * begin + offset
            else:
                spot = 2 * (begin + offset) + jnp.where(own_first, first, second)
            place = jnp.where(here, spot, place)
            left[edge] = left[edge] - size
            taken[edge] = taken[edge] + size
        mine = (begin <= me) & (me < begin + count)
        code = jnp.where(mine, sum(p << (3 * i) for i, p in enumerate(partner)), code)
        begin = begin + count
    slots = lax.broadcasted_iota(jnp.int32, (CHANNELS, CHANNELS), 0)
    perm_ref[...] = jnp.where(slots == place, 1.0, 0.0).astype(BF16)
    return jnp.max(code)


def put_back(part, perm):
    return lax.dot_general(part, perm[...], (((0,), (0,)), ((), ())), preferred_element_type=F32)


def kernel(
    ids_hbm, emb_hbm, gate_hbm, filt_hbm, comp_hbm, grad_hbm,
    outer_hbm, outer_back_hbm, inner_hbm, inner_back_hbm, twist_hbm,
    gate_out, recv_dk, perm_out,
    ids, emb, gate, filt, comp, grad,
    outer, outer_back, inner, inner_back, twist,
    perm, strided, letters, embedded, spectra_k, spectra_g, spectra_u,
    send_k, send_g, send_u, recv_k, recv_g, recv_u,
    send_du, send_dk, recv_du, gate_vmem,
    load_sem, store_sem, local_sem, send_sem, recv_sem,
):
    spectra = (spectra_k, spectra_g, spectra_u)
    seq, chan = lax.axis_index("seq"), lax.axis_index("chan")
    me = chan * SEQ_DEVICES + seq
    loads = {}
    sources = [
        (comp_hbm, comp), (ids_hbm, ids), (emb_hbm, emb), (filt_hbm, filt), (grad_hbm, grad), (gate_hbm, gate),
        (outer_hbm, outer), (twist_hbm, twist), (inner_hbm, inner), (inner_back_hbm, inner_back),
        (outer_back_hbm, outer_back),
    ]
    for index, (source, target) in enumerate(sources):
        loads[index] = pltpu.make_async_copy(source, target, load_sem.at[index])
        loads[index].start()

    barrier = pltpu.get_barrier_semaphore()

    near = Neighbours(seq, chan)
    near.each_other(
        lambda seq2, chan2: pl.semaphore_signal(barrier, inc=1, device_id=(seq2, chan2), device_id_type=MESH)
    )

    loads[0].wait()
    code = route(comp, seq, chan, perm)
    perm_store = pltpu.make_async_copy(perm, perm_out, store_sem.at[1])
    perm_store.start()

    def lay_out(source_of, target):
        for a in range(ROWS):
            strided[pl.ds(a, CHANNELS, stride=ROWS), :] = source_of(a)
        target[...] = strided[...].reshape(DEVICES, HALF, LANES).astype(BF16)

    def turned(ref):
        def part(a):
            block = ref[pl.ds(a * LANES, LANES), :]
            return lax.dot_general(perm[...], block, (((1,), (1,)), ((), ())), preferred_element_type=F32)
        return part

    def send_block(source, target, index, seq2, chan2):
        pltpu.make_async_remote_copy(
            source.at[chan2 * SEQ_DEVICES + seq2], target.at[me], send_sem.at[index], recv_sem.at[index],
            device_id=(seq2, chan2), device_id_type=MESH,
        ).start()

    def post(source, target, index):
        pltpu.make_async_copy(source.at[me], target.at[me], local_sem.at[index]).start()
        near.each_other(lambda seq2, chan2: send_block(source, target, index, seq2, chan2))

    def arrived(source, target, index):
        pltpu.make_async_copy(source.at[me], target.at[me], local_sem.at[index]).wait()
        rest = pl.ds(0, DEVICES - 1)
        pltpu.make_async_copy(target.at[rest], target.at[rest], recv_sem.at[index]).wait()

    def left_here(source, index):
        rest = pl.ds(0, DEVICES - 1)
        pltpu.make_async_copy(source.at[rest], source.at[rest], send_sem.at[index]).wait()

    loads[3].wait()
    lay_out(turned(filt), send_k)
    pl.semaphore_wait(barrier, DEVICES - 1)
    post(send_k, recv_k, 0)

    loads[4].wait()
    lay_out(turned(grad), send_g)

    loads[1].wait()
    loads[2].wait()
    names = lax.broadcasted_iota(jnp.int32, (4, ALL_CHANNELS), 0)
    letters[...] = jnp.where(names == ids[...], 1.0, 0.0).astype(BF16)
    own_emb = lax.dot_general(perm[...], emb[...], (((1,), (1,)), ((), ())), preferred_element_type=F32).astype(BF16)
    for a in range(ROWS):
        embedded[a] = jnp.dot(own_emb, letters[:, a * LANES : (a + 1) * LANES], preferred_element_type=F32)
    loads[5].wait()
    turn_gate = turned(gate)
    lay_out(lambda a: turn_gate(a) * embedded[a], send_u)

    post(send_g, recv_g, 1)

    for index in range(6, 11):
        loads[index].wait()

    def times(matrices, right):
        return jnp.dot(matrices[0], right, preferred_element_type=F32) + jnp.dot(
            matrices[1], right, preferred_element_type=F32
        )

    def times_right(left, matrices):
        return jnp.dot(left, matrices[0], preferred_element_type=F32) + jnp.dot(
            left, matrices[1], preferred_element_type=F32
        )

    def forward(received, shard):
        block = received[pl.ds(shard * SEQ_DEVICES, SEQ_DEVICES)].astype(F32)
        block = block.reshape(SEQ_DEVICES, 2, ROWS, LANES)
        fields = [block[:, slot].reshape(OUTER, INNER) for slot in range(2)]
        mixed = times(outer, jnp.concatenate(fields, axis=1).astype(BF16))
        cos, sin = twist[0], twist[1]
        spread = []
        for slot in range(2):
            real = mixed[:OUTER, slot * INNER : (slot + 1) * INNER]
            imag = mixed[OUTER:, slot * INNER : (slot + 1) * INNER]
            spread.append(jnp.concatenate([real * cos + imag * sin, imag * cos - real * sin], axis=1))
        return times_right(jnp.concatenate(spread, axis=0).astype(BF16), inner)

    def backward(parts):
        rows = [jnp.concatenate([real, imag], axis=1) for real, imag in parts]
        mixed = times_right(jnp.concatenate(rows, axis=0).astype(BF16), inner_back)
        cos, sin = twist[0], twist[1]
        spread = []
        for slot in range(2):
            real = mixed[slot * OUTER : (slot + 1) * OUTER, :INNER]
            imag = mixed[slot * OUTER : (slot + 1) * OUTER, INNER:]
            spread.append(jnp.concatenate([real * cos - imag * sin, imag * cos + real * sin], axis=0))
        fields = times(outer_back, jnp.concatenate(spread, axis=1).astype(BF16))
        halves = [
            fields[:, slot * INNER : (slot + 1) * INNER].reshape(SEQ_DEVICES, 1, ROWS, LANES) for slot in range(2)
        ]
        return jnp.concatenate(halves, axis=1).reshape(SEQ_DEVICES, HALF, LANES).astype(BF16)

    def spectrum(kind, channel):
        both = spectra[kind][channel]
        return both[:, :INNER], both[:, INNER:]

    def partner_of(channel):
        return lax.rem(lax.shift_right_logical(code, 3 * channel), SHARE)

    def forward_shard(received, kind, finish, shard):
        both = forward(received, shard)
        for slot in range(2):
            channel = 2 * shard + slot
            spectra[kind][channel] = finish(both[slot * OUTER : (slot + 1) * OUTER], channel)

    def all_forward(received, kind, finish):
        def body(shard, carry):
            forward_shard(received, kind, finish, shard)
            return carry

        lax.fori_loop(0, SHARDS, body, 0, unroll=UNROLL)

    def all_backward(combine, source, target, index):
        for other_core in (1, 0):
            core = lax.rem(near.core + other_core, 2)

            def body(z_high, carry):
                shard = 2 * z_high + core
                source[pl.ds(shard * SEQ_DEVICES, SEQ_DEVICES)] = backward([combine(2 * shard + slot) for slot in range(2)])
                return carry

            lax.fori_loop(0, 2, body, 0, unroll=True)
            near.each_in_half(other_core, lambda seq2, chan2: send_block(source, target, index, seq2, chan2))
        pltpu.make_async_copy(source.at[me], target.at[me], local_sem.at[index]).start()

    arrived(send_k, recv_k, 0)
    post(send_u, recv_u, 2)
    all_forward(recv_k, 0, lambda both, channel: both)
    arrived(send_g, recv_g, 1)

    def input_spectrum(channel):
        k_real, k_imag = spectrum(0, channel)
        p_real, p_imag = spectrum(0, partner_of(channel))
        g_real, g_imag = spectrum(1, channel)
        real, imag = k_real + p_real, p_imag - k_imag
        return g_real * real - g_imag * imag, g_real * imag + g_imag * real

    all_forward(recv_g, 1, lambda both, channel: both)
    all_backward(input_spectrum, send_du, recv_du, 3)

    def product(both, channel):
        g_real, g_imag = spectrum(1, channel)
        u_real, u_imag = both[:, :INNER], both[:, INNER:]
        return jnp.concatenate([g_real * u_real + g_imag * u_imag, g_imag * u_real - g_real * u_imag], axis=1)

    arrived(send_u, recv_u, 2)
    all_forward(recv_u, 2, product)

    def filter_spectrum(channel):
        real, imag = spectrum(2, channel)
        p_real, p_imag = spectrum(2, partner_of(channel))
        return real + p_real, imag - p_imag

    all_backward(filter_spectrum, send_dk, recv_dk, 4)

    arrived(send_du, recv_du, 3)
    strided[...] = recv_du[...].astype(F32).reshape(DEVICES * HALF, LANES)
    for a in range(ROWS):
        part = (strided[pl.ds(a, CHANNELS, stride=ROWS), :] * embedded[a]).astype(BF16)
        gate_vmem[pl.ds(a * LANES, LANES), :] = put_back(part, perm).astype(BF16)
    gate_store = pltpu.make_async_copy(gate_vmem, gate_out, store_sem.at[0])
    gate_store.start()
    arrived(send_dk, recv_dk, 4)
    for index, source in enumerate([send_k, send_g, send_u, send_du, send_dk]):
        left_here(source, index)
    gate_store.wait()
    perm_store.wait()


def finish(gate_hbm, back_hbm, perm_hbm, gate_out, filt_out, gate, back, perm, strided, filt, load_sem, store_sem):
    gate_load = pltpu.make_async_copy(gate_hbm, gate, load_sem.at[2])
    gate_store = pltpu.make_async_copy(gate, gate_out, store_sem.at[ROWS])
    back_load = pltpu.make_async_copy(back_hbm, back, load_sem.at[0])
    perm_load = pltpu.make_async_copy(perm_hbm, perm, load_sem.at[1])
    back_load.start()
    perm_load.start()
    gate_load.start()
    back_load.wait()
    strided[...] = back[...].astype(F32).reshape(DEVICES * HALF, LANES)
    gate_load.wait()
    gate_store.start()
    perm_load.wait()
    stores = []
    for a in range(ROWS):
        part = strided[pl.ds(a, CHANNELS, stride=ROWS), :].astype(BF16)
        rows = pl.ds(a * LANES, LANES)
        filt[rows, :] = put_back(part, perm)
        stores.append(pltpu.make_async_copy(filt.at[rows], filt_out.at[rows], store_sem.at[a]))
        stores[-1].start()
    for store in stores:
        store.wait()
    gate_store.wait()


def shards(base_ids, embedding, gate_values, filter_kernel, complement, output_gradient):
    positions, channels = filter_kernel.shape
    tables = transform_tables()
    blocks = pltpu.VMEM((DEVICES, HALF, LANES), BF16)
    parts = pl.pallas_call(
        kernel,
        out_shape=[
            jax.ShapeDtypeStruct((positions, channels), BF16),
            jax.ShapeDtypeStruct((DEVICES, HALF, LANES), BF16),
            jax.ShapeDtypeStruct((channels, channels), BF16),
        ],
        in_specs=[pl.BlockSpec(memory_space=pl.ANY)] * 11,
        out_specs=[pl.BlockSpec(memory_space=pl.ANY)] * 3,
        scratch_shapes=[
            pltpu.VMEM((1, positions), jnp.int32),
            pltpu.VMEM(embedding.shape, BF16),
            pltpu.VMEM((positions, channels), BF16),
            pltpu.VMEM((positions, channels), BF16),
            pltpu.VMEM((1, ALL_CHANNELS), jnp.int32),
            pltpu.VMEM((positions, channels), BF16),
            *[pltpu.VMEM(table.shape, table.dtype) for table in tables],
            pltpu.VMEM((channels, channels), BF16),
            pltpu.VMEM((DEVICES * HALF, LANES), F32),
            pltpu.VMEM((4, positions), BF16),
            pltpu.VMEM((ROWS, channels, LANES), F32),
            *[pltpu.VMEM((SHARE, OUTER, 2 * INNER), F32)] * 3,
            *[blocks] * 9,
            pltpu.VMEM((positions, channels), BF16),
            pltpu.SemaphoreType.DMA((11,)),
            pltpu.SemaphoreType.DMA((2,)),
            pltpu.SemaphoreType.DMA((5,)),
            pltpu.SemaphoreType.DMA((5,)),
            pltpu.SemaphoreType.DMA((5,)),
        ],
        compiler_params=pltpu.CompilerParams(collective_id=0, has_side_effects=True, vmem_limit_bytes=62 << 20),
        name="two_strand_gradients",
    )(
        base_ids, embedding, gate_values.reshape(positions, channels), filter_kernel,
        complement.reshape(1, -1), output_gradient.reshape(positions, channels),
        *[jnp.asarray(table) for table in tables],
    )
    gate_gradient, filter_gradient = pl.pallas_call(
        finish,
        out_shape=[
            jax.ShapeDtypeStruct((positions, channels), BF16),
            jax.ShapeDtypeStruct((positions, channels), F32),
        ],
        in_specs=[pl.BlockSpec(memory_space=pl.ANY)] * 3,
        out_specs=[pl.BlockSpec(memory_space=pl.ANY)] * 2,
        scratch_shapes=[
            pltpu.VMEM((positions, channels), BF16),
            blocks,
            pltpu.VMEM((channels, channels), BF16),
            pltpu.VMEM((DEVICES * HALF, LANES), F32),
            pltpu.VMEM((positions, channels), F32),
            pltpu.SemaphoreType.DMA((3,)),
            pltpu.SemaphoreType.DMA((ROWS + 1,)),
        ],
        compiler_params=pltpu.CompilerParams(vmem_limit_bytes=62 << 20),
        name="positions_by_channels",
    )(*parts)
    return gate_gradient[None], filter_gradient


def solution(mesh):
    in_specs = (
        P(None, "seq"),
        P(None, "chan"),
        P(None, "seq", "chan"),
        P("seq", "chan"),
        P(),
        P(None, "seq", "chan"),
    )
    out_specs = (P(None, "seq", "chan"), P("seq", "chan"))
    return jax.shard_map(shards, mesh=mesh, in_specs=in_specs, out_specs=out_specs, check_vma=False)
```

```python
import functools
import itertools
import math

import jax
import jax.numpy as jnp
import numpy as np
from jax import lax
from jax.experimental import pallas as pl
from jax.experimental.pallas import tpu as pltpu
from jax.sharding import PartitionSpec as P

MESH = pl.DeviceIdType.MESH
F32 = jnp.float32
BF16 = jnp.bfloat16
SHARDS = 4
SEQ_DEVICES = 32
DEVICES = SHARDS * SEQ_DEVICES
LANES = 128
ROWS = 8
LENGTH = 32768
SHARE = 2 * SHARDS
INNER = 128
OUTER = LENGTH // INNER
HALF = 2 * ROWS
CHANNELS = 256
ALL_CHANNELS = SHARDS * CHANNELS
UNROLL = 4


def two_factors():
    edges = [(a, b) for a in range(SHARDS) for b in range(a, SHARDS)]
    found = []
    for chosen in itertools.combinations_with_replacement(edges, SHARDS):
        degrees = [sum(edge.count(shard) for edge in chosen) for shard in range(SHARDS)]
        if degrees == [2] * SHARDS:
            found.append(chosen)
    return found


def slots_of(chosen):
    used = [0] * SHARDS
    ends = []
    partner = [0] * SHARE
    for a, b in chosen:
        first = used[a]
        used[a] += 1
        second = used[b]
        used[b] += 1
        ends.append((first, second))
        partner[2 * a + first] = 2 * b + second
        partner[2 * b + second] = 2 * a + first
    return ends, partner


FACTORS = [(chosen, *slots_of(chosen)) for chosen in two_factors()]


def split(table):
    high = table.astype(np.float32).astype(jnp.bfloat16)
    low = (table.astype(np.float32) - high.astype(np.float32)).astype(jnp.bfloat16)
    return np.stack([high, low])


def transform_tables():
    window = 2 * LENGTH
    k = np.arange(OUTER)[:, None] + 0.5
    outer_angle = 2 * np.pi * k * np.arange(OUTER)[None] / (2 * OUTER)
    outer = np.concatenate([np.cos(outer_angle), -np.sin(outer_angle)], axis=0)
    m = np.arange(INNER)
    inner_angle = 2 * np.pi * ((m[:, None] * m[None]) % INNER) / INNER
    c, s = np.cos(inner_angle), np.sin(inner_angle)
    inner = np.block([[c, -s], [s, c]])
    twist = 2 * np.pi * k * m[None] / window
    twists = np.stack([np.cos(twist), np.sin(twist)]).astype(np.float32)
    return split(outer), split(outer.T * (2.0 / window)), split(inner), split(inner.T), twists


FAR_FIRST = (2, 1, 3, 0)


class Neighbours:
    def __init__(self, seq, chan):
        self.sy, self.sz, self.sx = lax.div(seq, 8), lax.rem(lax.div(seq, 4), 2), lax.rem(seq, 4)
        self.sz_high, self.core = lax.div(chan, 2), lax.rem(chan, 2)
        self.x = [lax.rem(self.sx + step, 4) for step in range(4)]
        self.y = [lax.rem(self.sy + step, 4) * 8 for step in range(4)]

    def layer(self, step):
        z = lax.rem(self.sz_high * 2 + self.sz + lax.rem(step, 4), 4)
        core = lax.rem(self.core + lax.div(step, 4), 2)
        return lax.rem(z, 2) * 4, lax.div(z, 2) * 2 + core

    def each_in_half(self, other_core, visit):
        def around(step, own):
            low, chan = self.layer(step)
            for dy in FAR_FIRST:
                for dx in FAR_FIRST:
                    if not (own and dx == 0 and dy == 0):
                        visit(self.y[dy] + low + self.x[dx], chan)

        def body(step, carry):
            around(step, False)
            return carry

        if other_core:
            lax.fori_loop(4, 8, body, 0)
        else:
            lax.fori_loop(1, 4, body, 0)
            around(0, True)

    def each_other(self, visit):
        self.each_in_half(1, visit)
        self.each_in_half(0, visit)


def route(comp_ref, seq, chan, perm_ref):
    comp = comp_ref[...]
    every = lax.broadcasted_iota(jnp.int32, (1, ALL_CHANNELS), 1)
    low, high = jnp.minimum(comp, every), jnp.maximum(comp, every)
    kind = lax.div(low, CHANNELS) * SHARDS + lax.div(high, CHANNELS)
    kind = jnp.where(every < comp, kind, -1)
    kinds = lax.broadcasted_iota(jnp.int32, (16, ALL_CHANNELS), 0)
    hot = jnp.where(kinds == kind, 1.0, 0.0).astype(BF16)
    start = pl.multiple_of(chan * CHANNELS, CHANNELS)
    own_comp = comp_ref[:, pl.ds(start, CHANNELS)]
    own = lax.broadcasted_iota(jnp.int32, (1, CHANNELS), 1) + start
    own_low, own_high = jnp.minimum(own_comp, own), jnp.maximum(own_comp, own)
    own_first = own < own_comp
    own_kind = lax.div(own_low, CHANNELS) * SHARDS + lax.div(own_high, CHANNELS)
    before = lax.broadcasted_iota(jnp.int32, (ALL_CHANNELS, CHANNELS), 0) < own_low
    before = jnp.where(before, 1.0, 0.0).astype(BF16)
    ranks = jnp.dot(hot, before, preferred_element_type=F32)
    own_kinds = lax.broadcasted_iota(jnp.int32, (16, CHANNELS), 0) == own_kind
    rank = jnp.sum(jnp.where(own_kinds, ranks, 0.0), axis=0, keepdims=True)
    totals = jnp.dot(hot, jnp.ones((ALL_CHANNELS, CHANNELS), BF16), preferred_element_type=F32)
    rank = rank.astype(jnp.int32)
    totals = totals.astype(jnp.int32)
    left = {edge: totals[edge[0] * SHARDS + edge[1]][None] for edge in sorted({e for f in FACTORS for e in f[0]})}
    taken = {edge: jnp.zeros((1, CHANNELS), jnp.int32) for edge in left}
    begin = jnp.zeros((1, CHANNELS), jnp.int32)
    me = chan * SEQ_DEVICES + seq
    place = jnp.zeros((1, CHANNELS), jnp.int32)
    code = jnp.zeros((1, CHANNELS), jnp.int32)
    for chosen, ends, partner in FACTORS:
        count = None
        for edge in sorted(set(chosen)):
            possible = left[edge] if chosen.count(edge) == 1 else lax.shift_right_logical(left[edge], 1)
            count = possible if count is None else jnp.minimum(count, possible)
        for edge in sorted(set(chosen)):
            times = chosen.count(edge)
            first, second = ends[chosen.index(edge)]
            offset = rank - taken[edge]
            size = count * times
            here = (own_kind == edge[0] * SHARDS + edge[1]) & (offset >= 0) & (offset < size)
            if times == 2:
                spot = 2 * begin + offset
            else:
                spot = 2 * (begin + offset) + jnp.where(own_first, first, second)
            place = jnp.where(here, spot, place)
            left[edge] = left[edge] - size
            taken[edge] = taken[edge] + size
        mine = (begin <= me) & (me < begin + count)
        code = jnp.where(mine, sum(p << (3 * i) for i, p in enumerate(partner)), code)
        begin = begin + count
    slots = lax.broadcasted_iota(jnp.int32, (CHANNELS, CHANNELS), 0)
    perm_ref[...] = jnp.where(slots == place, 1.0, 0.0).astype(BF16)
    return jnp.max(code)


def put_back(part, perm):
    return lax.dot_general(part, perm[...], (((0,), (0,)), ((), ())), preferred_element_type=F32)


def kernel(
    ids_hbm, emb_hbm, gate_hbm, filt_hbm, comp_hbm, grad_hbm,
    outer_hbm, outer_back_hbm, inner_hbm, inner_back_hbm, twist_hbm,
    gate_out, recv_dk, perm_out,
    ids, emb, gate, filt, comp, grad,
    outer, outer_back, inner, inner_back, twist,
    perm, strided, letters, embedded, spectra_k, spectra_g, spectra_u,
    send_k, send_g, send_u, recv_k, recv_g, recv_u,
    send_du, send_dk, recv_du, gate_vmem,
    load_sem, store_sem, local_sem, send_sem, recv_sem,
):
    spectra = (spectra_k, spectra_g, spectra_u)
    seq, chan = lax.axis_index("seq"), lax.axis_index("chan")
    me = chan * SEQ_DEVICES + seq
    loads = {}
    sources = [
        (comp_hbm, comp), (ids_hbm, ids), (emb_hbm, emb), (filt_hbm, filt), (grad_hbm, grad), (gate_hbm, gate),
        (outer_hbm, outer), (twist_hbm, twist), (inner_hbm, inner), (inner_back_hbm, inner_back),
        (outer_back_hbm, outer_back),
    ]
    for index, (source, target) in enumerate(sources):
        loads[index] = pltpu.make_async_copy(source, target, load_sem.at[index])
    for index in (0, 3):
        loads[index].start()

    barrier = pltpu.get_barrier_semaphore()

    near = Neighbours(seq, chan)
    near.each_other(
        lambda seq2, chan2: pl.semaphore_signal(barrier, inc=1, device_id=(seq2, chan2), device_id_type=MESH)
    )

    for index in (4, 1, 2, 5, 6, 7, 8, 9, 10):
        loads[index].start()

    loads[0].wait()
    code = route(comp, seq, chan, perm)
    perm_store = pltpu.make_async_copy(perm, perm_out, store_sem.at[1])
    perm_store.start()

    def lay_out(source_of, target):
        for a in range(ROWS):
            strided[pl.ds(a, CHANNELS, stride=ROWS), :] = source_of(a)
        target[...] = strided[...].reshape(DEVICES, HALF, LANES).astype(BF16)

    def turned(ref):
        def part(a):
            block = ref[pl.ds(a * LANES, LANES), :]
            return lax.dot_general(perm[...], block, (((1,), (1,)), ((), ())), preferred_element_type=F32)
        return part

    def send_block(source, target, index, seq2, chan2):
        pltpu.make_async_remote_copy(
            source.at[chan2 * SEQ_DEVICES + seq2], target.at[me], send_sem.at[index], recv_sem.at[index],
            device_id=(seq2, chan2), device_id_type=MESH,
        ).start()

    def post(source, target, index):
        pltpu.make_async_copy(source.at[me], target.at[me], local_sem.at[index]).start()
        near.each_other(lambda seq2, chan2: send_block(source, target, index, seq2, chan2))

    def arrived(source, target, index):
        pltpu.make_async_copy(source.at[me], target.at[me], local_sem.at[index]).wait()
        rest = pl.ds(0, DEVICES - 1)
        pltpu.make_async_copy(target.at[rest], target.at[rest], recv_sem.at[index]).wait()

    def left_here(source, index):
        rest = pl.ds(0, DEVICES - 1)
        pltpu.make_async_copy(source.at[rest], source.at[rest], send_sem.at[index]).wait()

    loads[3].wait()
    lay_out(turned(filt), send_k)
    pl.semaphore_wait(barrier, DEVICES - 1)
    post(send_k, recv_k, 0)

    loads[4].wait()
    lay_out(turned(grad), send_g)

    loads[1].wait()
    loads[2].wait()
    names = lax.broadcasted_iota(jnp.int32, (4, ALL_CHANNELS), 0)
    letters[...] = jnp.where(names == ids[...], 1.0, 0.0).astype(BF16)
    own_emb = lax.dot_general(perm[...], emb[...], (((1,), (1,)), ((), ())), preferred_element_type=F32).astype(BF16)
    for a in range(ROWS):
        embedded[a] = jnp.dot(own_emb, letters[:, a * LANES : (a + 1) * LANES], preferred_element_type=F32)
    loads[5].wait()
    turn_gate = turned(gate)
    lay_out(lambda a: turn_gate(a) * embedded[a], send_u)

    post(send_g, recv_g, 1)

    for index in range(6, 11):
        loads[index].wait()

    def times(matrices, right):
        return jnp.dot(matrices[0], right, preferred_element_type=F32) + jnp.dot(
            matrices[1], right, preferred_element_type=F32
        )

    def times_right(left, matrices):
        return jnp.dot(left, matrices[0], preferred_element_type=F32) + jnp.dot(
            left, matrices[1], preferred_element_type=F32
        )

    def forward(received, shard):
        block = received[pl.ds(shard * SEQ_DEVICES, SEQ_DEVICES)].astype(F32)
        block = block.reshape(SEQ_DEVICES, 2, ROWS, LANES)
        fields = [block[:, slot].reshape(OUTER, INNER) for slot in range(2)]
        mixed = times(outer, jnp.concatenate(fields, axis=1).astype(BF16))
        cos, sin = twist[0], twist[1]
        spread = []
        for slot in range(2):
            real = mixed[:OUTER, slot * INNER : (slot + 1) * INNER]
            imag = mixed[OUTER:, slot * INNER : (slot + 1) * INNER]
            spread.append(jnp.concatenate([real * cos + imag * sin, imag * cos - real * sin], axis=1))
        return times_right(jnp.concatenate(spread, axis=0).astype(BF16), inner)

    def backward(parts):
        rows = [jnp.concatenate([real, imag], axis=1) for real, imag in parts]
        mixed = times_right(jnp.concatenate(rows, axis=0).astype(BF16), inner_back)
        cos, sin = twist[0], twist[1]
        spread = []
        for slot in range(2):
            real = mixed[slot * OUTER : (slot + 1) * OUTER, :INNER]
            imag = mixed[slot * OUTER : (slot + 1) * OUTER, INNER:]
            spread.append(jnp.concatenate([real * cos - imag * sin, imag * cos + real * sin], axis=0))
        fields = times(outer_back, jnp.concatenate(spread, axis=1).astype(BF16))
        halves = [
            fields[:, slot * INNER : (slot + 1) * INNER].reshape(SEQ_DEVICES, 1, ROWS, LANES) for slot in range(2)
        ]
        return jnp.concatenate(halves, axis=1).reshape(SEQ_DEVICES, HALF, LANES).astype(BF16)

    def spectrum(kind, channel):
        both = spectra[kind][channel]
        return both[:, :INNER], both[:, INNER:]

    def partner_of(channel):
        return lax.rem(lax.shift_right_logical(code, 3 * channel), SHARE)

    def forward_shard(received, kind, finish, shard):
        both = forward(received, shard)
        for slot in range(2):
            channel = 2 * shard + slot
            spectra[kind][channel] = finish(both[slot * OUTER : (slot + 1) * OUTER], channel)

    def all_forward(received, kind, finish):
        def body(shard, carry):
            forward_shard(received, kind, finish, shard)
            return carry

        lax.fori_loop(0, SHARDS, body, 0, unroll=UNROLL)

    def all_backward(combine, source, target, index):
        for other_core in (1, 0):
            core = lax.rem(near.core + other_core, 2)

            def body(z_high, carry):
                shard = 2 * z_high + core
                source[pl.ds(shard * SEQ_DEVICES, SEQ_DEVICES)] = backward([combine(2 * shard + slot) for slot in range(2)])
                return carry

            lax.fori_loop(0, 2, body, 0, unroll=True)
            near.each_in_half(other_core, lambda seq2, chan2: send_block(source, target, index, seq2, chan2))
        pltpu.make_async_copy(source.at[me], target.at[me], local_sem.at[index]).start()

    arrived(send_k, recv_k, 0)
    post(send_u, recv_u, 2)
    all_forward(recv_k, 0, lambda both, channel: both)
    arrived(send_g, recv_g, 1)

    def input_spectrum(channel):
        k_real, k_imag = spectrum(0, channel)
        p_real, p_imag = spectrum(0, partner_of(channel))
        g_real, g_imag = spectrum(1, channel)
        real, imag = k_real + p_real, p_imag - k_imag
        return g_real * real - g_imag * imag, g_real * imag + g_imag * real

    all_forward(recv_g, 1, lambda both, channel: both)
    all_backward(input_spectrum, send_du, recv_du, 3)

    def product(both, channel):
        g_real, g_imag = spectrum(1, channel)
        u_real, u_imag = both[:, :INNER], both[:, INNER:]
        return jnp.concatenate([g_real * u_real + g_imag * u_imag, g_imag * u_real - g_real * u_imag], axis=1)

    arrived(send_u, recv_u, 2)
    all_forward(recv_u, 2, product)

    def filter_spectrum(channel):
        real, imag = spectrum(2, channel)
        p_real, p_imag = spectrum(2, partner_of(channel))
        return real + p_real, imag - p_imag

    all_backward(filter_spectrum, send_dk, recv_dk, 4)

    arrived(send_du, recv_du, 3)
    strided[...] = recv_du[...].astype(F32).reshape(DEVICES * HALF, LANES)
    for a in range(ROWS):
        part = (strided[pl.ds(a, CHANNELS, stride=ROWS), :] * embedded[a]).astype(BF16)
        gate_vmem[pl.ds(a * LANES, LANES), :] = put_back(part, perm).astype(BF16)
    gate_store = pltpu.make_async_copy(gate_vmem, gate_out, store_sem.at[0])
    gate_store.start()
    arrived(send_dk, recv_dk, 4)
    for index, source in enumerate([send_k, send_g, send_u, send_du, send_dk]):
        left_here(source, index)
    gate_store.wait()
    perm_store.wait()


def finish(gate_hbm, back_hbm, perm_hbm, gate_out, filt_out, gate, back, perm, strided, filt, load_sem, store_sem):
    gate_load = pltpu.make_async_copy(gate_hbm, gate, load_sem.at[2])
    gate_store = pltpu.make_async_copy(gate, gate_out, store_sem.at[ROWS])
    back_load = pltpu.make_async_copy(back_hbm, back, load_sem.at[0])
    perm_load = pltpu.make_async_copy(perm_hbm, perm, load_sem.at[1])
    back_load.start()
    perm_load.start()
    gate_load.start()
    back_load.wait()
    strided[...] = back[...].astype(F32).reshape(DEVICES * HALF, LANES)
    gate_load.wait()
    gate_store.start()
    perm_load.wait()
    stores = []
    for a in range(ROWS):
        part = strided[pl.ds(a, CHANNELS, stride=ROWS), :].astype(BF16)
        rows = pl.ds(a * LANES, LANES)
        filt[rows, :] = put_back(part, perm)
        stores.append(pltpu.make_async_copy(filt.at[rows], filt_out.at[rows], store_sem.at[a]))
        stores[-1].start()
    for store in stores:
        store.wait()
    gate_store.wait()


def shards(base_ids, embedding, gate_values, filter_kernel, complement, output_gradient):
    positions, channels = filter_kernel.shape
    tables = transform_tables()
    blocks = pltpu.VMEM((DEVICES, HALF, LANES), BF16)
    parts = pl.pallas_call(
        kernel,
        out_shape=[
            jax.ShapeDtypeStruct((positions, channels), BF16),
            jax.ShapeDtypeStruct((DEVICES, HALF, LANES), BF16),
            jax.ShapeDtypeStruct((channels, channels), BF16),
        ],
        in_specs=[pl.BlockSpec(memory_space=pl.ANY)] * 11,
        out_specs=[pl.BlockSpec(memory_space=pl.ANY)] * 3,
        scratch_shapes=[
            pltpu.VMEM((1, positions), jnp.int32),
            pltpu.VMEM(embedding.shape, BF16),
            pltpu.VMEM((positions, channels), BF16),
            pltpu.VMEM((positions, channels), BF16),
            pltpu.VMEM((1, ALL_CHANNELS), jnp.int32),
            pltpu.VMEM((positions, channels), BF16),
            *[pltpu.VMEM(table.shape, table.dtype) for table in tables],
            pltpu.VMEM((channels, channels), BF16),
            pltpu.VMEM((DEVICES * HALF, LANES), F32),
            pltpu.VMEM((4, positions), BF16),
            pltpu.VMEM((ROWS, channels, LANES), F32),
            *[pltpu.VMEM((SHARE, OUTER, 2 * INNER), F32)] * 3,
            *[blocks] * 9,
            pltpu.VMEM((positions, channels), BF16),
            pltpu.SemaphoreType.DMA((11,)),
            pltpu.SemaphoreType.DMA((2,)),
            pltpu.SemaphoreType.DMA((5,)),
            pltpu.SemaphoreType.DMA((5,)),
            pltpu.SemaphoreType.DMA((5,)),
        ],
        compiler_params=pltpu.CompilerParams(collective_id=0, has_side_effects=True, vmem_limit_bytes=62 << 20),
        name="two_strand_gradients",
    )(
        base_ids, embedding, gate_values.reshape(positions, channels), filter_kernel,
        complement.reshape(1, -1), output_gradient.reshape(positions, channels),
        *[jnp.asarray(table) for table in tables],
    )
    gate_gradient, filter_gradient = pl.pallas_call(
        finish,
        out_shape=[
            jax.ShapeDtypeStruct((positions, channels), BF16),
            jax.ShapeDtypeStruct((positions, channels), F32),
        ],
        in_specs=[pl.BlockSpec(memory_space=pl.ANY)] * 3,
        out_specs=[pl.BlockSpec(memory_space=pl.ANY)] * 2,
        scratch_shapes=[
            pltpu.VMEM((positions, channels), BF16),
            blocks,
            pltpu.VMEM((channels, channels), BF16),
            pltpu.VMEM((DEVICES * HALF, LANES), F32),
            pltpu.VMEM((positions, channels), F32),
            pltpu.SemaphoreType.DMA((3,)),
            pltpu.SemaphoreType.DMA((ROWS + 1,)),
        ],
        compiler_params=pltpu.CompilerParams(vmem_limit_bytes=62 << 20),
        name="positions_by_channels",
    )(*parts)
    return gate_gradient[None], filter_gradient


def solution(mesh):
    in_specs = (
        P(None, "seq"),
        P(None, "chan"),
        P(None, "seq", "chan"),
        P("seq", "chan"),
        P(),
        P(None, "seq", "chan"),
    )
    out_specs = (P(None, "seq", "chan"), P("seq", "chan"))
    return jax.shard_map(shards, mesh=mesh, in_specs=in_specs, out_specs=out_specs, check_vma=False)
```
